256 devices in a mesh: docs: 32 (over y, x, core), grp: 8 (over z).
Axes of the slice: x: 4, y: 4, z: 8, core: 2. Of those that a mesh axis runs over, the one named last changes fastest.
Arguments:
- embeds: bfloat16 [65536, 1024], P('docs'), may hold values from -300 to 300
- cluster_of: int32 [65536], P('docs'), may hold values from 0 to 31, as said below
Outputs:
- nearest: float32 [65536], P('docs')
The draws below stay inside these ranges and needn't reach their ends.
Inputs may be any that keep to these rules, and one draw needn't show every extreme that they name: `cluster_of`: each document names one cluster. The 2048 documents of one docs shard name no cluster more than 128 times and some cluster exactly 128 times; every cluster is named by 128 or more documents.
All inputs are finite; a program needn't handle non-finite values.
Results may differ from the reference program's by a relative error of at most 0.0005.
Values may be sent and summed in bfloat16 or wider, within the bound.
A program may use at most 64 MiB of HBM per device.

```python
import math
import jax
import jax.numpy as jnp
from jax import lax

W = 1024
ROWS_DEV = 2048
CLUSTERS = 32
SLOT = 128
CAP = 4096
DOCS = 65536


def assign(key):
    key = jax.random.fold_in(key, 101)
    blocks = DOCS // ROWS_DEV
    offset_key, priority_key, jitter_key, shuffle_key = jax.random.split(key, 4)
    offset = jax.random.randint(offset_key, (), 0, CLUSTERS)
    priorities = jax.random.randint(priority_key, (CLUSTERS,), 0, 4)
    slot_cluster = jnp.arange(CAP, dtype=jnp.int32) // SLOT
    favored = (jnp.arange(blocks, dtype=jnp.int32) + offset) % CLUSTERS
    priority = jnp.where(slot_cluster[None, :] == favored[:, None], 0, priorities[slot_cluster][None, :] + 1)
    jitter = jax.random.randint(jitter_key, (blocks, CAP), 0, 1024)
    sort_key = (priority * 1024 + jitter) * CAP + jnp.arange(CAP, dtype=jnp.int32)[None, :]
    chosen = jnp.argsort(sort_key, axis=1)[:, :ROWS_DEV]
    clusters = (chosen // SLOT).astype(jnp.int32)
    shuffle = jax.random.randint(shuffle_key, (blocks, ROWS_DEV), 0, 4096) * ROWS_DEV + jnp.arange(ROWS_DEV, dtype=jnp.int32)[None, :]
    row_order = jnp.argsort(shuffle, axis=1)
    return jnp.take_along_axis(clusters, row_order, axis=1).reshape(-1).astype(jnp.int32)


def draw_cluster_of(key, part):
    clusters = assign(key)
    return clusters


def draw_embeds(key, part):
    clusters = assign(key)
    key = jax.random.fold_in(key, 7)
    noise_key, pair_key, scale_key, order_key, centre_key, weight_key = jax.random.split(key, 6)
    onehot = (clusters[:, None] == jnp.arange(CLUSTERS, dtype=jnp.int32)[None, :]).astype(jnp.int32)
    counts = jnp.sum(onehot, axis=0)
    starts = (jnp.cumsum(counts) - counts).astype(jnp.int32)
    shuffled = jax.random.permutation(order_key, DOCS).astype(jnp.int32)
    order_key_values = clusters * DOCS + shuffled
    order = jnp.argsort(order_key_values).astype(jnp.int32)
    sorted_position = jnp.zeros((DOCS,), jnp.int32).at[order].set(jnp.arange(DOCS, dtype=jnp.int32))
    within = sorted_position - starts[clusters]
    pair_id = clusters * DOCS + within // 2

    def shared(number):
        inner_key = jax.random.fold_in(pair_key, number)
        vector_key, strength_key, live_key = jax.random.split(inner_key, 3)
        vector = jax.random.normal(vector_key, (W,), jnp.float32)
        strength = jax.random.uniform(strength_key, (), jnp.float32, 0.3, 0.95)
        live = jax.random.randint(live_key, (), 0, 2)
        return (vector, jnp.where(live > 0, strength, 0.0))
    vectors, strength = jax.vmap(shared)(pair_id)

    def centre(number):
        return jax.random.normal(jax.random.fold_in(centre_key, number), (W,), jnp.float32)
    centres = jax.vmap(centre)(jnp.arange(CLUSTERS, dtype=jnp.int32))
    weight = jax.random.uniform(weight_key, (DOCS,), jnp.float32, 0.05, 0.55)
    private = jax.random.normal(noise_key, (DOCS, W), jnp.float32)
    lowest_scale = 1.0
    highest_scale = 10.0
    scales = jnp.exp(jax.random.uniform(scale_key, (DOCS, 1), jnp.float32, math.log(lowest_scale), math.log(highest_scale)))
    pair_weight = strength * (1.0 - weight)
    private_weight = (1.0 - strength) * (1.0 - weight)
    blended = jnp.sqrt(private_weight)[:, None] * private + jnp.sqrt(pair_weight)[:, None] * vectors + jnp.sqrt(weight)[:, None] * centres[clusters]
    return (blended * scales).astype(jnp.bfloat16)


def setup_inputs(seed: int = 0) -> dict:
    key_list = jax.random.split(jax.random.key(seed), 3)
    return {
        "embeds": draw_embeds(jax.random.fold_in(key_list[2], 71), 0),
        "cluster_of": draw_cluster_of(jax.random.fold_in(key_list[2], 71), 0),
    }


EPSILON = 1e-06
LOWEST = -3e+38

def normalize(embeds):
    values = embeds.astype(jnp.float32)
    inverse = lax.rsqrt(lax.optimization_barrier(jnp.sum(values * values, axis=1, keepdims=True)) + EPSILON)
    return (values * inverse).astype(jnp.bfloat16)

def cluster_rank(cluster_of, cluster_count):
    onehot = (cluster_of[:, None] == jnp.arange(cluster_count, dtype=jnp.int32)[None, :]).astype(jnp.int32)
    earlier = jnp.cumsum(onehot, axis=0) - onehot
    return lax.optimization_barrier(jnp.sum(earlier * onehot, axis=1)).astype(jnp.int32)

def reference(embeds, cluster_of):
    doc_count = embeds.shape[0]
    unit_rows = normalize(embeds)
    member_rank = cluster_rank(cluster_of, CLUSTERS)
    position = (cluster_of * CAP + member_rank).astype(jnp.int32)
    slot_table = jnp.full((CLUSTERS * CAP,), doc_count, jnp.int32)
    slot_table = slot_table.at[position].set(jnp.arange(doc_count, dtype=jnp.int32)).reshape(CLUSTERS, CAP)
    padded = jnp.concatenate([unit_rows, jnp.zeros((1, unit_rows.shape[1]), jnp.bfloat16)], axis=0)

    def one_cluster(members):
        member_rows = padded[members].astype(jnp.float32)
        similarity = jnp.dot(member_rows, member_rows.T, precision=lax.Precision.HIGHEST, preferred_element_type=jnp.float32)
        allowed = (members[None, :] < doc_count) & (members[:, None] != members[None, :])
        return lax.optimization_barrier(jnp.max(jnp.where(allowed, similarity, LOWEST), axis=1))
    nearest_slot = lax.map(one_cluster, slot_table).reshape(-1)
    return nearest_slot[position]
```

```python
import jax
import jax.numpy as jnp
from jax import lax
from jax.experimental import pallas as pl
from jax.experimental.pallas import tpu as pltpu
from jax.sharding import PartitionSpec as P


EPSILON = 1e-06
LOWEST = -3e38
FAR = -1e30
PADDED = 2.0

SIDE = 4
PLANES = 8
DOCS = 2048
WIDTH = 1024
SLOTS = 128
STAGES = 4
PIECE = SLOTS // STAGES
SOURCES = 16
HALF = SOURCES * PIECE
STAGE_ROWS = 2 * HALF
MEMBERS = STAGES * STAGE_ROWS
COLS = 256
LINES = DOCS // 128

MESH = pl.DeviceIdType.MESH
F32 = jnp.float32
BF16 = jnp.bfloat16
NT = (((1,), (1,)), ((), ()))


def iota(shape, axis):
    return lax.broadcasted_iota(jnp.int32, shape, axis)


def kernel(
    cluster_ref, embeds_ref, out_ref,
    rows, pick, gathered, blocks, relay, members, row_bias, col_bias, row_max, col_max, row_best, answer,
    returned, partial, lane_of, line_of,
    load_sem, sent, relay_arrive, forwarded, arrive, swap_sent, swap_arrive, back_sent, back_arrive,
    part_sent, part_arrive,
):
    docs = lax.axis_index("docs")
    z = lax.axis_index("grp")
    core = lax.rem(docs, 2)
    x = lax.rem(lax.div(docs, 2), SIDE)
    y = lax.div(docs, 2 * SIDE)
    role = lax.rem(x - y + z + SIDE, SIDE)
    sibling = docs + 1 - 2 * core
    v = lax.rem(y - z + PLANES, SIDE)

    def place(px, py, pcore):
        return (lax.rem(py, SIDE) * SIDE + lax.rem(px, SIDE)) * 2 + pcore

    def plane(pz):
        return lax.rem(pz + PLANES, PLANES)

    target = [place(v, y, core), place(v + 3, y + 3, core), place(v + 1, y + 2, core), place(v + 2, y + 1, core)]
    home = [z, z, plane(z + 1), plane(z - 1)]
    number = [SIDE * home[b] + lax.rem(y + SIDE - b, SIDE) for b in range(4)]
    column = [role, lax.rem(role + 1, SIDE), lax.rem(role + 3, SIDE), lax.rem(role + 2, SIDE)]

    load = pltpu.make_async_copy(embeds_ref, rows, load_sem)
    load.start()

    barrier = pltpu.get_barrier_semaphore()

    def greet(device):
        pl.semaphore_signal(barrier, inc=1, device_id=device, device_id_type=MESH)

    greet((sibling, z))
    for step in range(1, PLANES):
        greet((docs, plane(z + step)))

    @pl.when(role == 0)
    def _():
        for dx in range(1, SIDE):
            greet((place(x + dx, y, core), z))
        for dx in range(SIDE):
            greet((place(x + dx, y + 1, core), z))

    @pl.when((role == 3) | (role == 1))
    def _():
        for dx in range(SIDE):
            greet((place(x + dx, y + 2 + lax.div(3 - role, 2), core), z))

    clusters = cluster_ref[...]
    member = [jnp.where(clusters == number[b], 1.0, 0.0).astype(F32) for b in range(4)]
    stacked = jnp.concatenate(member, axis=0).astype(BF16)
    before = jnp.where(iota((128, 128), 0) < iota((128, 128), 1), 1.0, 0.0).astype(BF16)
    within = jnp.dot(stacked, before, preferred_element_type=F32)
    totals = jnp.dot(stacked, jnp.ones((128, 128), BF16), preferred_element_type=F32)
    lines = 4 * LINES
    above = (iota((lines, lines), 1) < iota((lines, lines), 0)) & (
        lax.div(iota((lines, lines), 1), LINES) == lax.div(iota((lines, lines), 0), LINES)
    )
    offsets = jnp.dot(jnp.where(above, 1.0, 0.0).astype(BF16), totals.astype(BF16), preferred_element_type=F32)
    rank = within + offsets

    slot = iota((SLOTS, 128), 0).astype(F32)
    lane_sum = jnp.full((LINES, 128), -1.0, F32)
    line_sum = jnp.full((LINES, 128), -1.0, F32)
    counts = []
    for b in range(4):
        mine = rank[b * LINES : (b + 1) * LINES]
        position = jnp.where(member[b] > 0, mine, -1.0)
        for r in range(LINES):
            pick[b * SLOTS : (b + 1) * SLOTS, r * 128 : (r + 1) * 128] = jnp.where(
                slot == position[r : r + 1], 1.0, 0.0
            ).astype(BF16)
        counts.append(jnp.sum(totals[b * LINES : (b + 1) * LINES], axis=0, keepdims=True))
        stage = jnp.floor(mine * (1.0 / PIECE))
        shift = (column[b] * PIECE).astype(F32)
        lane_sum = jnp.where(member[b] > 0, mine - stage * PIECE + shift, lane_sum)
        line_sum = jnp.where(member[b] > 0, stage + b * STAGES, line_sum)
    lane_of[...] = lane_sum
    line_of[...] = line_sum

    load.wait()

    def gather(n, carry):
        cols = pl.ds(pl.multiple_of(n * COLS, COLS), COLS)
        gathered[:, cols] = jnp.dot(pick[...], rows[:, cols], preferred_element_type=F32)
        return carry

    lax.fori_loop(0, WIDTH // COLS, gather, 0)

    for b in range(4):
        span = slice(b * SLOTS, (b + 1) * SLOTS)
        values = gathered[span, :]
        inverse = lax.rsqrt(jnp.sum(values * values, axis=1, keepdims=True) + EPSILON)
        unit = (values * inverse).astype(BF16)
        blocks[span, :] = unit
        empty = (slot >= counts[b]) & (iota((SLOTS, 128), 1) == 0)
        head = values[:, 0:128] * inverse
        blocks[span, 0:128] = jnp.where(empty, PADDED, head).astype(BF16)

    @pl.when(role == 0)
    def _():
        pl.semaphore_wait(barrier, PLANES + 3)

    @pl.when(role != 0)
    def _():
        pl.semaphore_wait(barrier, PLANES + 4)

    def member_rows(t, half, source):
        return members.at[pl.ds(pl.multiple_of(t * STAGE_ROWS + half * HALF + source * PIECE, PIECE), PIECE)]

    def relay_rows(t, dx):
        return relay.at[pl.ds(pl.multiple_of((t * SIDE + dx) * PIECE, PIECE), PIECE)]

    def block_rows(t, b):
        return blocks.at[pl.ds(pl.multiple_of(b * SLOTS + t * PIECE, PIECE), PIECE)]

    def send(t, b):
        if b < 2:
            dst = member_rows(t, core, SIDE * b + column[b])
            sem = arrive.at[t, SIDE * b + column[b]]
        else:
            dst = relay_rows(t, column[b])
            sem = relay_arrive.at[t, column[b]]
        return pltpu.make_async_remote_copy(
            src_ref=block_rows(t, b), dst_ref=dst, send_sem=sent.at[t, b], recv_sem=sem,
            device_id=(target[b], z), device_id_type=MESH,
        )

    def keep(t):
        return pltpu.make_async_copy(block_rows(t, 0), member_rows(t, core, 0), arrive.at[t, 0])

    def start_sends(t):
        send(t, 3).start()
        send(t, 2).start()
        send(t, 1).start()

        @pl.when(role != 0)
        def _():
            send(t, 0).start()

        @pl.when(role == 0)
        def _():
            keep(t).start()

    def end_sends(t):
        send(t, 3).wait_send()
        send(t, 2).wait_send()
        send(t, 1).wait_send()

        @pl.when(role != 0)
        def _():
            send(t, 0).wait_send()

    row_of_relay = 2 + lax.div(3 - role, 2)
    plane_of_relay = lax.rem(z + 1 + (3 - role) * 3, PLANES)

    def forward(t, dx):
        source = SIDE * row_of_relay + dx
        return pltpu.make_async_remote_copy(
            src_ref=relay_rows(t, dx), dst_ref=member_rows(t, core, source),
            send_sem=forwarded.at[t, dx], recv_sem=arrive.at[t, source],
            device_id=(docs, plane_of_relay), device_id_type=MESH,
        )

    def arrival(t, source):
        return pltpu.make_async_copy(member_rows(t, core, source), member_rows(t, core, source), arrive.at[t, source])

    def relay_arrival(t, dx):
        return pltpu.make_async_copy(relay_rows(t, dx), relay_rows(t, dx), relay_arrive.at[t, dx])

    def swap(t, half):
        span = pl.ds(pl.multiple_of(t * STAGE_ROWS + half * HALF, HALF), HALF)
        return pltpu.make_async_remote_copy(
            src_ref=members.at[span], dst_ref=members.at[span], send_sem=swap_sent.at[t], recv_sem=swap_arrive.at[t],
            device_id=(sibling, z), device_id_type=MESH,
        )

    start_sends(0)
    start_sends(1)

    @pl.when(role == 0)
    def _():
        col_max[...] = jnp.full(col_max.shape, LOWEST, F32)
        answer[...] = jnp.full(answer.shape, LOWEST, F32)

    def compute(t):
        base = pl.multiple_of(t * STAGE_ROWS + core * HALF, HALF)
        first = members[pl.ds(base, HALF), 0:128].astype(F32)[:, 0:1]
        row_bias[...] = jnp.broadcast_to(jnp.where(first > 1.5, FAR, 0.0), (HALF, 128))
        row_max[...] = jnp.full(row_max.shape, LOWEST, F32)

        def scores(start):
            return lax.dot_general(
                members[pl.ds(base, HALF), :], members[pl.ds(start, COLS), :], NT, preferred_element_type=F32
            )

        def along_rows(score, bias):
            biased = score + bias
            best = row_max[...]
            for c in range(0, COLS, 128):
                best = jnp.maximum(best, biased[:, c : c + 128])
            row_max[...] = best

        def old(n, carry):
            start = pl.multiple_of(n * COLS, COLS)
            score = scores(start)
            along_rows(score, col_bias[0:1, pl.ds(start, COLS)])
            for c in range(0, COLS, 128):
                biased = (score[:, c : c + 128] + row_bias[...]).reshape(HALF // 8, 8, 128)
                cols = pl.ds(pl.multiple_of(start + c, 128), 128)
                col_max[:, cols] = jnp.maximum(col_max[:, cols], jnp.max(biased, axis=0))
            return carry

        def mark(start):
            chosen = jnp.where((iota((16, 128), 0) < 8) & (iota((16, 128), 1) == 0), 1.0, 0.0).astype(BF16)
            heads = lax.dot_general(chosen, members[pl.ds(start, COLS), 0:128], NT, preferred_element_type=F32)
            bias = jnp.where(heads[0:8] > 1.5, FAR, 0.0)
            col_bias[:, pl.ds(start, COLS)] = bias
            return bias[0:1]

        def own(n, carry):
            start = pl.multiple_of(base + n * COLS, COLS)
            same = iota((HALF, COLS), 0) == iota((HALF, COLS), 1) + n * COLS
            along_rows(jnp.where(same, LOWEST, scores(start)), mark(start))
            return carry

        def other(n, carry):
            start = pl.multiple_of(t * STAGE_ROWS + (1 - core) * HALF + n * COLS, COLS)
            along_rows(scores(start), mark(start))
            return carry

        lax.fori_loop(0, t * (STAGE_ROWS // COLS), old, 0)
        lax.fori_loop(0, HALF // COLS, own, 0)
        swap(t, 1 - core).wait_recv()
        lax.fori_loop(0, HALF // COLS, other, 0)
        for dy in range(SIDE):
            turned = row_max[dy * 128 : (dy + 1) * 128, :].T
            row_best[pl.ds(t * SIDE + dy, 1), :] = jnp.max(turned, axis=0, keepdims=True)

    def stage_body(t, carry):
        @pl.when((role == 3) | (role == 1))
        def _():
            for dx in range(SIDE):
                relay_arrival(t, dx).wait()
                forward(t, dx).start()

        @pl.when(role == 0)
        def _():
            for source in range(SOURCES):
                arrival(t, source).wait()
            swap(t, core).start()
            compute(t)

        end_sends(t)

        @pl.when(t + 2 < STAGES)
        def _():
            start_sends(t + 2)

        return carry

    lax.fori_loop(0, STAGES, stage_body, 0)

    source_plane = [z, z, plane(z - 1), plane(z + 1)]

    def give(half, dy, dx, device):
        return pltpu.make_async_remote_copy(
            src_ref=answer.at[half, dy], dst_ref=returned.at[dy, core],
            send_sem=back_sent.at[half, dy, dx], recv_sem=back_arrive.at[dy, core],
            device_id=(device, source_plane[dy]), device_id_type=MESH,
        )

    def gives():
        copies = [give(1 - core, 0, 0, sibling)]
        for dy in range(SIDE):
            for dx in range(SIDE):
                if dx or dy:
                    for half in range(2):
                        copies.append(give(half, dy, dx, place(x + dx, y + dy, half)))
        return copies

    @pl.when(role == 0)
    def _():
        for t in range(STAGES):
            for half in range(2):
                for dy in range(SIDE):
                    start = t * STAGE_ROWS + half * HALF + dy * 128
                    best = jnp.max(col_max[:, start : start + 128], axis=0, keepdims=True)
                    mine = row_best[t * SIDE + dy : t * SIDE + dy + 1, :]
                    answer[half, dy, t : t + 1] = jnp.where(core == half, jnp.maximum(best, mine), best)
        for copy in gives():
            copy.start()
        pltpu.make_async_copy(answer.at[core, 0], returned.at[0, core], back_arrive.at[0, core]).start()

    for b in range(4):
        for half in range(2):
            pltpu.make_async_copy(returned.at[b, half], returned.at[b, half], back_arrive.at[b, half]).wait()

    found = jnp.concatenate(
        [jnp.maximum(returned[b, 0], returned[b, 1])[0:STAGES] for b in range(4)], axis=0
    )
    high = found.astype(BF16)
    rest = found - high.astype(F32)
    middle = rest.astype(BF16)
    low = (rest - middle.astype(F32)).astype(BF16)
    parts = jnp.concatenate([high, middle, low], axis=0)
    lane = iota((128, 128), 0).astype(F32)
    line = iota((16, 128), 0).astype(F32)
    for r in range(LINES):
        chosen = jnp.where(lane == lane_of[r : r + 1, :], 1.0, 0.0).astype(BF16)
        taken = jnp.dot(parts, chosen, preferred_element_type=F32)
        taken = taken[0:16] + taken[16:32] + taken[32:48]
        partial[z, r : r + 1] = jnp.sum(
            jnp.where(line == line_of[r : r + 1, :], taken, 0.0), axis=0, keepdims=True
        )

    def share(step):
        return pltpu.make_async_remote_copy(
            src_ref=partial.at[z], dst_ref=partial.at[z],
            send_sem=part_sent.at[step], recv_sem=part_arrive.at[step],
            device_id=(docs, plane(z + step)), device_id_type=MESH,
        )

    for step in range(1, PLANES):
        share(step).start()
    for step in range(1, PLANES):
        slot_of = partial.at[plane(z - step)]
        pltpu.make_async_copy(slot_of, slot_of, part_arrive.at[step]).wait()
    total = partial[0]
    for step in range(1, PLANES):
        total = total + partial[step]
    out_ref[...] = total

    for step in range(1, PLANES):
        share(step).wait_send()

    @pl.when((role == 3) | (role == 1))
    def _():
        for t in range(STAGES):
            for dx in range(SIDE):
                forward(t, dx).wait_send()

    @pl.when(role == 0)
    def _():
        for t in range(STAGES):
            swap(t, core).wait_send()
        for copy in gives():
            copy.wait_send()


def local(embeds, cluster_of):
    dma = pltpu.SemaphoreType.DMA
    out = pl.pallas_call(
        kernel,
        out_shape=jax.ShapeDtypeStruct((LINES, 128), F32),
        in_specs=[pl.BlockSpec(memory_space=pltpu.VMEM), pl.BlockSpec(memory_space=pl.ANY)],
        out_specs=pl.BlockSpec(memory_space=pltpu.VMEM),
        scratch_shapes=[
            pltpu.VMEM((DOCS, WIDTH), BF16),
            pltpu.VMEM((4 * SLOTS, DOCS), BF16),
            pltpu.VMEM((4 * SLOTS, WIDTH), F32),
            pltpu.VMEM((4 * SLOTS, WIDTH), BF16),
            pltpu.VMEM((4 * SLOTS, WIDTH), BF16),
            pltpu.VMEM((MEMBERS, WIDTH), BF16),
            pltpu.VMEM((HALF, 128), F32),
            pltpu.VMEM((8, MEMBERS), F32),
            pltpu.VMEM((HALF, 128), F32),
            pltpu.VMEM((8, MEMBERS), F32),
            pltpu.VMEM((STAGES * SIDE, 128), F32),
            pltpu.VMEM((2, SIDE, 8, 128), F32),
            pltpu.VMEM((4, 2, 8, 128), F32),
            pltpu.VMEM((PLANES, LINES, 128), F32),
            pltpu.VMEM((LINES, 128), F32),
            pltpu.VMEM((LINES, 128), F32),
            dma,
            dma((STAGES, 4)),
            dma((STAGES, SIDE)),
            dma((STAGES, SIDE)),
            dma((STAGES, SOURCES)),
            dma((STAGES,)),
            dma((STAGES,)),
            dma((2, SIDE, SIDE)),
            dma((4, 2)),
            dma((PLANES,)),
            dma((PLANES,)),
        ],
        compiler_params=pltpu.CompilerParams(
            collective_id=0, has_side_effects=True, vmem_limit_bytes=48 * 2**20
        ),
        cost_estimate=pl.CostEstimate(flops=13 * 10**9, bytes_accessed=4 * 2**20, transcendentals=512),
    )(cluster_of.reshape(LINES, 128), embeds)
    return out.reshape(DOCS)


def solution(mesh):
    return jax.shard_map(
        local,
        mesh=mesh,
        in_specs=(P("docs", None), P("docs")),
        out_specs=P("docs"),
        check_vma=False,
    )
```

```python
import jax
import jax.numpy as jnp
from jax import lax
from jax.experimental import pallas as pl
from jax.experimental.pallas import tpu as pltpu
from jax.sharding import PartitionSpec as P


EPSILON = 1e-06
LOWEST = -3e38
FAR = -1e30
PADDED = 2.0

SIDE = 4
PLANES = 8
DOCS = 2048
WIDTH = 1024
SLOTS = 128
STAGES = 4
PIECE = SLOTS // STAGES
GROUP = SIDE * PIECE
STAGE_ROWS = 4 * GROUP
MEMBERS = STAGES * STAGE_ROWS
COLS = 256
LINES = DOCS // 128
OTHER, OWN, NEXT, PREVIOUS = range(4)

MESH = pl.DeviceIdType.MESH
F32 = jnp.float32
BF16 = jnp.bfloat16
NT = (((1,), (1,)), ((), ()))


def iota(shape, axis):
    return lax.broadcasted_iota(jnp.int32, shape, axis)


def kernel(
    cluster_ref, embeds_ref, out_ref,
    rows, pick, gathered, blocks, members, row_bias, col_bias, row_max, col_max, row_best, answer,
    returned, partial, lane_of, line_of,
    load_sem, shipped, arrive, passed, near_arrive, swap_sent, swap_arrive, back_sent, back_arrive,
    part_sent, part_arrive, hello,
):
    docs = lax.axis_index("docs")
    z = lax.axis_index("grp")
    core = lax.rem(docs, 2)
    x = lax.rem(lax.div(docs, 2), SIDE)
    y = lax.div(docs, 2 * SIDE)

    def place(px, py, pcore):
        return (lax.rem(py + SIDE, SIDE) * SIDE + lax.rem(px, SIDE)) * 2 + lax.rem(pcore, 2)

    def plane(pz):
        return lax.rem(pz + PLANES, PLANES)

    def turn(py):
        return lax.div(lax.rem(py + 3, SIDE), 2)

    sibling = place(x, y, core + 1)
    ahead = place(x, y + 1, core + turn(y + 1))
    behind = place(x, y - 1, core)
    from_ahead = place(x, y + 1, core)
    from_behind = place(x, y - 1, core + turn(y))

    load = pltpu.make_async_copy(embeds_ref, rows, load_sem)
    load.start()

    barrier = pltpu.get_barrier_semaphore()

    def greet(device):
        pl.semaphore_signal(barrier, inc=1, device_id=device, device_id_type=MESH)

    for step in range(1, SIDE):
        greet((place(x + step, y, core), z))
    greet((from_ahead, z))
    greet((from_behind, z))
    greet((sibling, z))
    greet((docs, plane(z + 1)))
    greet((docs, plane(z - 1)))

    clusters = cluster_ref[...]
    member = [jnp.where(clusters == SIDE * z + b, 1.0, 0.0).astype(F32) for b in range(4)]
    stacked = jnp.concatenate(member, axis=0).astype(BF16)
    before = jnp.where(iota((128, 128), 0) < iota((128, 128), 1), 1.0, 0.0).astype(BF16)
    within = jnp.dot(stacked, before, preferred_element_type=F32)
    totals = jnp.dot(stacked, jnp.ones((128, 128), BF16), preferred_element_type=F32)
    lines = 4 * LINES
    above = (iota((lines, lines), 1) < iota((lines, lines), 0)) & (
        lax.div(iota((lines, lines), 1), LINES) == lax.div(iota((lines, lines), 0), LINES)
    )
    offsets = jnp.dot(jnp.where(above, 1.0, 0.0).astype(BF16), totals.astype(BF16), preferred_element_type=F32)
    rank = within + offsets

    slot = iota((SLOTS, 128), 0).astype(F32)
    lane_sum = jnp.full((LINES, 128), -1.0, F32)
    line_sum = jnp.full((LINES, 128), -1.0, F32)
    counts = []
    for b in range(4):
        mine = rank[b * LINES : (b + 1) * LINES]
        position = jnp.where(member[b] > 0, mine, -1.0)
        for r in range(LINES):
            pick[b * SLOTS : (b + 1) * SLOTS, r * 128 : (r + 1) * 128] = jnp.where(
                slot == position[r : r + 1], 1.0, 0.0
            ).astype(BF16)
        counts.append(jnp.sum(totals[b * LINES : (b + 1) * LINES], axis=0, keepdims=True))
        stage = jnp.floor(mine * (1.0 / PIECE))
        lane_sum = jnp.where(member[b] > 0, mine - stage * PIECE + (x * PIECE).astype(F32), lane_sum)
        line_sum = jnp.where(member[b] > 0, stage + b * STAGES, line_sum)
    lane_of[...] = lane_sum
    line_of[...] = line_sum

    load.wait()

    def gather(n, carry):
        cols = pl.ds(pl.multiple_of(n * COLS, COLS), COLS)
        gathered[:, cols] = jnp.dot(pick[...], rows[:, cols], preferred_element_type=F32)
        return carry

    lax.fori_loop(0, WIDTH // COLS, gather, 0)

    for b in range(4):
        span = slice(b * SLOTS, (b + 1) * SLOTS)
        values = gathered[span, :]
        inverse = lax.rsqrt(jnp.sum(values * values, axis=1, keepdims=True) + EPSILON)
        unit = (values * inverse).astype(BF16)
        blocks[span, :] = unit
        empty = (slot >= counts[b]) & (iota((SLOTS, 128), 1) == 0)
        head = values[:, 0:128] * inverse
        blocks[span, 0:128] = jnp.where(empty, PADDED, head).astype(BF16)

    pl.semaphore_wait(barrier, SIDE + 4)

    def group_rows(t, group):
        return pl.ds(pl.multiple_of(t * STAGE_ROWS + group * GROUP, GROUP), GROUP)

    def piece(t, group, source):
        return members.at[pl.ds(pl.multiple_of(t * STAGE_ROWS + group * GROUP + source * PIECE, PIECE), PIECE)]

    def block(t, b):
        return blocks.at[pl.ds(pl.multiple_of(b * SLOTS + t * PIECE, PIECE), PIECE)]

    def arrival(ref, sem):
        return pltpu.make_async_copy(ref, ref, sem)

    def ship(t, step):
        column = lax.rem(x + step, SIDE)
        return pltpu.make_async_remote_copy(
            src_ref=block(t, column), dst_ref=piece(t, OWN, x),
            send_sem=shipped.at[t, step], recv_sem=arrive.at[t, x],
            device_id=(place(column, y, core), z), device_id_type=MESH,
        )

    def pass_on(t, source, src, group):
        return pltpu.make_async_remote_copy(
            src_ref=src, dst_ref=piece(t, group, source),
            send_sem=passed.at[t, source, group - NEXT], recv_sem=near_arrive.at[t, source, group - NEXT],
            device_id=(behind if group == NEXT else ahead, z), device_id_type=MESH,
        )

    def pass_both(t, source, src):
        pass_on(t, source, src, NEXT).start()
        pass_on(t, source, src, PREVIOUS).start()

    def swap(t):
        return pltpu.make_async_remote_copy(
            src_ref=members.at[group_rows(t, OWN)], dst_ref=members.at[group_rows(t, OTHER)],
            send_sem=swap_sent.at[t], recv_sem=swap_arrive.at[t],
            device_id=(sibling, z), device_id_type=MESH,
        )

    def start_ships(t):
        pass_both(t, x, block(t, x))
        for step in (2, 3, 1):
            ship(t, step).start()
        pltpu.make_async_copy(block(t, x), piece(t, OWN, x), arrive.at[t, x]).start()

    def end_ships(t):
        for step in (2, 3, 1):
            ship(t, step).wait_send()

    def relay(t):
        for step in (3, 1, 2):
            source = lax.rem(x + step, SIDE)
            arrival(piece(t, OWN, source), arrive.at[t, source]).wait()
            pass_both(t, source, piece(t, OWN, source))
        arrival(piece(t, OWN, x), arrive.at[t, x]).wait()
        swap(t).start()

    def compute(t):
        base = pl.multiple_of(t * STAGE_ROWS, STAGE_ROWS)
        first = members[pl.ds(base, STAGE_ROWS), 0:128].astype(F32)[:, 0:1]
        row_bias[...] = jnp.broadcast_to(jnp.where(first > 1.5, FAR, 0.0), (STAGE_ROWS, 128))
        row_max[...] = jnp.full(row_max.shape, LOWEST, F32)

        def scores(start):
            return lax.dot_general(
                members[pl.ds(base, STAGE_ROWS), :], members[pl.ds(start, COLS), :], NT, preferred_element_type=F32
            )

        def along_rows(score, bias):
            biased = score + bias
            best = row_max[...]
            for c in range(0, COLS, 128):
                best = jnp.maximum(best, biased[:, c : c + 128])
            row_max[...] = best

        def old(n, carry):
            start = pl.multiple_of(n * COLS, COLS)
            score = scores(start)
            along_rows(score, col_bias[0:1, pl.ds(start, COLS)])
            for c in range(0, COLS, 128):
                biased = (score[:, c : c + 128] + row_bias[...]).reshape(STAGE_ROWS // 8, 8, 128)
                cols = pl.ds(pl.multiple_of(start + c, 128), 128)
                col_max[:, cols] = jnp.maximum(col_max[:, cols], jnp.max(biased, axis=0))
            return carry

        def mark(start):
            chosen = jnp.where((iota((16, 128), 0) < 8) & (iota((16, 128), 1) == 0), 1.0, 0.0).astype(BF16)
            heads = lax.dot_general(chosen, members[pl.ds(start, COLS), 0:128], NT, preferred_element_type=F32)
            bias = jnp.where(heads[0:8] > 1.5, FAR, 0.0)
            col_bias[:, pl.ds(start, COLS)] = bias
            return bias[0:1]

        def new(n, carry):
            start = pl.multiple_of(base + n * COLS, COLS)
            same = iota((STAGE_ROWS, COLS), 0) == iota((STAGE_ROWS, COLS), 1) + n * COLS
            along_rows(jnp.where(same, LOWEST, scores(start)), mark(start))
            return carry

        lax.fori_loop(0, t * (STAGE_ROWS // COLS), old, 0)
        lax.fori_loop(0, STAGE_ROWS // COLS, new, 0)
        for group in range(4):
            turned = row_max[group * GROUP : (group + 1) * GROUP, :].T
            row_best[pl.ds(t * 4 + group, 1), :] = jnp.max(turned, axis=0, keepdims=True)

    start_ships(0)
    start_ships(1)
    col_max[...] = jnp.full(col_max.shape, LOWEST, F32)
    answer[...] = jnp.full(answer.shape, LOWEST, F32)

    for turn_of in range(3):
        for step in (1, -1):
            pl.semaphore_signal(hello.at[turn_of], inc=1, device_id=(docs, plane(z + step)), device_id_type=MESH)
        pl.semaphore_wait(hello.at[turn_of], 2)

    relay(0)

    def stage_body(t, carry):
        end_ships(t)

        @pl.when(t + 2 < STAGES)
        def _():
            start_ships(t + 2)

        @pl.when(t + 1 < STAGES)
        def _():
            relay(t + 1)

        for source in range(SIDE):
            for group in (NEXT, PREVIOUS):
                arrival(piece(t, group, source), near_arrive.at[t, source, group - NEXT]).wait()
        swap(t).wait_recv()
        compute(t)
        return carry

    lax.fori_loop(0, STAGES, stage_body, 0)

    for t in range(STAGES):
        for group in range(4):
            start = t * STAGE_ROWS + group * GROUP
            best = jnp.max(col_max[:, start : start + GROUP], axis=0, keepdims=True)
            mine = row_best[t * 4 + group : t * 4 + group + 1, :]
            answer[group, t : t + 1] = jnp.maximum(best, mine)

    def give(group, step):
        column = x + step
        device = [
            place(column, y, core + 1), place(column, y, core),
            place(column, y + 1, core), place(column, y - 1, core + turn(y)),
        ][group]
        return pltpu.make_async_remote_copy(
            src_ref=answer.at[group], dst_ref=returned.at[x, group],
            send_sem=back_sent.at[group, step], recv_sem=back_arrive.at[x, group],
            device_id=(device, z), device_id_type=MESH,
        )

    gives = [give(group, step) for step in (2, 1, 3, 0) for group in range(4) if step or group != OWN]
    for copy in gives:
        copy.start()
    pltpu.make_async_copy(answer.at[OWN], returned.at[x, OWN], back_arrive.at[x, OWN]).start()
    for b in range(4):
        for group in range(4):
            arrival(returned.at[b, group], back_arrive.at[b, group]).wait()

    found = jnp.concatenate(
        [
            jnp.maximum(
                jnp.maximum(returned[b, 0], returned[b, 1]), jnp.maximum(returned[b, 2], returned[b, 3])
            )[0:STAGES]
            for b in range(4)
        ],
        axis=0,
    )
    high = found.astype(BF16)
    rest = found - high.astype(F32)
    middle = rest.astype(BF16)
    low = (rest - middle.astype(F32)).astype(BF16)
    parts = jnp.concatenate([high, middle, low], axis=0)
    lane = iota((128, 128), 0).astype(F32)
    line = iota((16, 128), 0).astype(F32)
    for r in range(LINES):
        chosen = jnp.where(lane == lane_of[r : r + 1, :], 1.0, 0.0).astype(BF16)
        taken = jnp.dot(parts, chosen, preferred_element_type=F32)
        taken = taken[0:16] + taken[16:32] + taken[32:48]
        partial[z, r : r + 1] = jnp.sum(
            jnp.where(line == line_of[r : r + 1, :], taken, 0.0), axis=0, keepdims=True
        )

    def share(step):
        return pltpu.make_async_remote_copy(
            src_ref=partial.at[z], dst_ref=partial.at[z],
            send_sem=part_sent.at[step], recv_sem=part_arrive.at[step],
            device_id=(docs, plane(z + step)), device_id_type=MESH,
        )

    for step in range(1, PLANES):
        share(step).start()
    for step in range(1, PLANES):
        slot_of = partial.at[plane(z - step)]
        pltpu.make_async_copy(slot_of, slot_of, part_arrive.at[step]).wait()
    total = partial[0]
    for step in range(1, PLANES):
        total = total + partial[step]
    out_ref[...] = total

    for step in range(1, PLANES):
        share(step).wait_send()

    for copy in gives:
        copy.wait_send()

    def end_stage(t, carry):
        swap(t).wait_send()
        for source in range(SIDE):
            for group in (NEXT, PREVIOUS):
                pass_on(t, source, piece(t, OWN, source), group).wait_send()
        return carry

    lax.fori_loop(0, STAGES, end_stage, 0)


def local(embeds, cluster_of):
    dma = pltpu.SemaphoreType.DMA
    out = pl.pallas_call(
        kernel,
        out_shape=jax.ShapeDtypeStruct((LINES, 128), F32),
        in_specs=[pl.BlockSpec(memory_space=pltpu.VMEM), pl.BlockSpec(memory_space=pl.ANY)],
        out_specs=pl.BlockSpec(memory_space=pltpu.VMEM),
        scratch_shapes=[
            pltpu.VMEM((DOCS, WIDTH), BF16),
            pltpu.VMEM((4 * SLOTS, DOCS), BF16),
            pltpu.VMEM((4 * SLOTS, WIDTH), F32),
            pltpu.VMEM((4 * SLOTS, WIDTH), BF16),
            pltpu.VMEM((MEMBERS, WIDTH), BF16),
            pltpu.VMEM((STAGE_ROWS, 128), F32),
            pltpu.VMEM((8, MEMBERS), F32),
            pltpu.VMEM((STAGE_ROWS, 128), F32),
            pltpu.VMEM((8, MEMBERS), F32),
            pltpu.VMEM((STAGES * 4, 128), F32),
            pltpu.VMEM((4, 8, 128), F32),
            pltpu.VMEM((4, 4, 8, 128), F32),
            pltpu.VMEM((PLANES, LINES, 128), F32),
            pltpu.VMEM((LINES, 128), F32),
            pltpu.VMEM((LINES, 128), F32),
            dma,
            dma((STAGES, SIDE)),
            dma((STAGES, SIDE)),
            dma((STAGES, SIDE, 2)),
            dma((STAGES, SIDE, 2)),
            dma((STAGES,)),
            dma((STAGES,)),
            dma((4, SIDE)),
            dma((4, 4)),
            dma((PLANES,)),
            dma((PLANES,)),
            pltpu.SemaphoreType.REGULAR((3,)),
        ],
        compiler_params=pltpu.CompilerParams(
            collective_id=0, has_side_effects=True, vmem_limit_bytes=48 * 2**20
        ),
        cost_estimate=pl.CostEstimate(flops=8 * 10**9, bytes_accessed=4 * 2**20, transcendentals=512),
    )(cluster_of.reshape(LINES, 128), embeds)
    return out.reshape(DOCS)


def solution(mesh):
    return jax.shard_map(
        local,
        mesh=mesh,
        in_specs=(P("docs", None), P("docs")),
        out_specs=P("docs"),
        check_vma=False,
    )
```

```python
import jax
import jax.numpy as jnp
from jax import lax
from jax.experimental import pallas as pl
from jax.experimental.pallas import tpu as pltpu
from jax.sharding import PartitionSpec as P


EPSILON = 1e-06
LOWEST = -3e38
FAR = -1e30
PADDED = 2.0

SIDE = 4
PLANES = 8
CLUSTERS = SIDE * PLANES
DOCS = 2048
WIDTH = 1024
SLOTS = 128
STAGES = 4
PIECE = SLOTS // STAGES
GROUP = SIDE * PIECE
REGION = STAGES * GROUP
MEMBERS = 4 * REGION
EARLY = PIECE
LINES = DOCS // 128
OWN, OTHER, PREVIOUS, NEXT = range(4)

MESH = pl.DeviceIdType.MESH
F32 = jnp.float32
BF16 = jnp.bfloat16
NT = (((1,), (1,)), ((), ()))


def iota(shape, axis):
    return lax.broadcasted_iota(jnp.int32, shape, axis)


def kernel(
    cluster_ref, embeds_ref, out_ref,
    rows, pick, gathered, blocks, members, col_bias, row_max, col_max, answer,
    near, final, returned, rank_of,
    load_sem, shipped, arrive, passed, near_arrive, swap_sent, swap_arrive, near_sent, back_near, back_sent,
    back_arrive, hello,
):
    docs = lax.axis_index("docs")
    z = lax.axis_index("grp")
    core = lax.rem(docs, 2)
    x = lax.rem(lax.div(docs, 2), SIDE)
    y = lax.div(docs, 2 * SIDE)

    def place(px, py, pcore):
        return (lax.rem(py + SIDE, SIDE) * SIDE + lax.rem(px, SIDE)) * 2 + lax.rem(pcore, 2)

    def plane(pz):
        return lax.rem(pz + PLANES, PLANES)

    def turn(py):
        return lax.div(lax.rem(py + 3, SIDE), 2)

    sibling = place(x, y, core + 1)
    ahead = place(x, y + 1, core + turn(y + 1))
    behind = place(x, y - 1, core)
    from_ahead = place(x, y + 1, core)
    from_behind = place(x, y - 1, core + turn(y))

    load = pltpu.make_async_copy(embeds_ref, rows, load_sem)
    load.start()

    barrier = pltpu.get_barrier_semaphore()

    def greet(device):
        pl.semaphore_signal(barrier, inc=1, device_id=device, device_id_type=MESH)

    for step in range(1, SIDE):
        greet((place(x + step, y, core), z))
    greet((from_ahead, z))
    greet((from_behind, z))
    greet((sibling, z))
    greet((docs, plane(z + 1)))
    greet((docs, plane(z - 1)))

    clusters = cluster_ref[...]

    def ranks(numbers):
        member = [jnp.where(clusters == number, 1.0, 0.0).astype(F32) for number in numbers]
        stacked = jnp.concatenate(member, axis=0).astype(BF16)
        before = jnp.where(iota((128, 128), 0) < iota((128, 128), 1), 1.0, 0.0).astype(BF16)
        within = jnp.dot(stacked, before, preferred_element_type=F32)
        totals = jnp.dot(stacked, jnp.ones((128, 128), BF16), preferred_element_type=F32)
        lines = len(member) * LINES
        above = (iota((lines, lines), 1) < iota((lines, lines), 0)) & (
            lax.div(iota((lines, lines), 1), LINES) == lax.div(iota((lines, lines), 0), LINES)
        )
        offsets = jnp.dot(
            jnp.where(above, 1.0, 0.0).astype(BF16), totals.astype(BF16), preferred_element_type=F32
        )
        return member, within + offsets, totals

    member, rank, totals = ranks([SIDE * z + b for b in range(4)])
    positions = [jnp.where(member[b] > 0, rank[b * LINES : (b + 1) * LINES], -1.0) for b in range(4)]
    counts = [jnp.sum(totals[b * LINES : (b + 1) * LINES], axis=0, keepdims=True) for b in range(4)]

    def mark_slots(low, high):
        size = high - low
        slot = iota((size, 128), 0).astype(F32) + low
        for b in range(4):
            for r in range(LINES):
                pick[b * size : (b + 1) * size, r * 128 : (r + 1) * 128] = jnp.where(
                    slot == positions[b][r : r + 1], 1.0, 0.0
                ).astype(BF16)

    def take_slots(low, high):
        size = high - low

        def gather(n, carry):
            cols = pl.ds(pl.multiple_of(n * 256, 256), 256)
            gathered[0 : 4 * size, cols] = jnp.dot(
                pick[0 : 4 * size, :], rows[:, cols], preferred_element_type=F32
            )
            return carry

        lax.fori_loop(0, WIDTH // 256, gather, 0)
        slot = iota((size, 128), 0).astype(F32) + low
        for b in range(4):
            values = gathered[b * size : (b + 1) * size, :]
            inverse = lax.rsqrt(jnp.sum(values * values, axis=1, keepdims=True) + EPSILON)
            scaled = values * inverse
            empty = (slot >= counts[b]) & (iota((size, 128), 1) == 0)
            head = jnp.where(empty, PADDED, scaled[:, 0:128]).astype(BF16)
            unit = scaled.astype(BF16)
            for part in range(0, size, PIECE):
                at = ((low + part) // PIECE * 4 + b) * PIECE
                blocks[at : at + PIECE, :] = unit[part : part + PIECE]
                blocks[at : at + PIECE, 0:128] = head[part : part + PIECE]

    mark_slots(0, EARLY)
    load.wait()
    take_slots(0, EARLY)
    pl.semaphore_wait(barrier, SIDE + 4)

    def piece(t, group, source):
        return members.at[pl.ds(pl.multiple_of(group * REGION + t * GROUP + source * PIECE, PIECE), PIECE)]

    def block(t, b):
        return blocks.at[pl.ds(pl.multiple_of((t * 4 + b) * PIECE, PIECE), PIECE)]

    def arrival(ref, sem):
        return pltpu.make_async_copy(ref, ref, sem)

    def ship(t, step):
        column = lax.rem(x + step, SIDE)
        return pltpu.make_async_remote_copy(
            src_ref=block(t, column), dst_ref=piece(t, OWN, x),
            send_sem=shipped.at[t, step], recv_sem=arrive.at[t, x],
            device_id=(place(column, y, core), z), device_id_type=MESH,
        )

    def pass_on(t, source, src, group):
        return pltpu.make_async_remote_copy(
            src_ref=src, dst_ref=piece(t, group, source),
            send_sem=passed.at[t, source, group - PREVIOUS], recv_sem=near_arrive.at[t, source, group - PREVIOUS],
            device_id=(behind if group == NEXT else ahead, z), device_id_type=MESH,
        )

    def pass_both(t, source, src):
        pass_on(t, source, src, NEXT).start()
        pass_on(t, source, src, PREVIOUS).start()

    def swap(t):
        return pltpu.make_async_remote_copy(
            src_ref=members.at[pl.ds(OWN * REGION + t * GROUP, GROUP)],
            dst_ref=members.at[pl.ds(OTHER * REGION + t * GROUP, GROUP)],
            send_sem=swap_sent.at[t], recv_sem=swap_arrive.at[t],
            device_id=(sibling, z), device_id_type=MESH,
        )

    def start_ships(t):
        for step in (2, 3, 1):
            ship(t, step).start()

    def end_ships(t):
        for step in (2, 3, 1):
            ship(t, step).wait_send()

    def keep(t):
        pass_both(t, x, block(t, x))
        pltpu.make_async_copy(block(t, x), piece(t, OWN, x), arrive.at[t, x]).start()

    def relay(t):
        for step in (3, 1, 2):
            source = lax.rem(x + step, SIDE)
            arrival(piece(t, OWN, source), arrive.at[t, source]).wait()
            pass_both(t, source, piece(t, OWN, source))
        arrival(piece(t, OWN, x), arrive.at[t, x]).wait()
        swap(t).start()

    def await_near(t):
        for source in range(SIDE):
            for group in (NEXT, PREVIOUS):
                arrival(piece(t, group, source), near_arrive.at[t, source, group - PREVIOUS]).wait()

    def tell(step):
        for way in (1, -1):
            pl.semaphore_signal(hello.at[step], inc=1, device_id=(docs, plane(z + way)), device_id_type=MESH)

    def mark(start, size):
        chosen = jnp.where((iota((16, 128), 0) < 8) & (iota((16, 128), 1) == 0), 1.0, 0.0).astype(BF16)
        heads = lax.dot_general(chosen, members[start : start + size, 0:128], NT, preferred_element_type=F32)
        col_bias[:, start : start + size] = jnp.where(heads[0:8] > 1.5, FAR, 0.0)

    def bias_of_rows(start, size):
        first = members[start : start + size, 0:128].astype(F32)[:, 0:1]
        return jnp.where(first > 1.5, FAR, 0.0)

    def scores(base, size, start, width):
        return lax.dot_general(
            members[base : base + size, :], members[start : start + width, :], NT, preferred_element_type=F32
        )

    def along_rows(best, score, start, width):
        biased = score + col_bias[0:1, start : start + width]
        for c in range(0, width, 128):
            best = jnp.maximum(best, biased[:, c : c + 128])
        return best

    def turned(best):
        return jnp.max(best.T, axis=0, keepdims=True)

    def pair_own():
        row_max[...] = jnp.full((REGION, 128), LOWEST, F32)
        for n in range(2 * REGION // 256):
            start = n * 256
            mark(start, 256)
            score = scores(0, REGION, start, 256)
            if start < REGION:
                score = jnp.where(iota((REGION, 256), 0) == iota((REGION, 256), 1) + start, LOWEST, score)
            row_max[...] = along_rows(row_max[...], score, start, 256)
        for t in range(STAGES):
            answer[OWN, t : t + 1] = turned(row_max[t * GROUP : (t + 1) * GROUP, :])

    def pair(base, start, stop):
        bias = bias_of_rows(base, GROUP)
        best = jnp.full((GROUP, 128), LOWEST, F32)
        while start < stop:
            width = min(512, stop - start)
            score = scores(base, GROUP, start, width)
            best = along_rows(best, score, start, width)
            biased = (score + bias).reshape(GROUP // 8, 8, width)
            span = slice(start, start + width)
            col_max[:, span] = jnp.maximum(col_max[:, span], jnp.max(biased, axis=0))
            start += width
        return turned(best)

    def pair_near(t):
        nexts, previous = NEXT * REGION + t * GROUP, PREVIOUS * REGION + t * GROUP
        mark(previous, GROUP)
        answer[NEXT, t : t + 1] = pair(nexts, 0, previous + GROUP)
        if t:
            answer[PREVIOUS, t : t + 1] = pair(previous, NEXT * REGION, nexts)
        if t + 1 < STAGES:
            mark(nexts, GROUP)

    def hear(step):
        pl.semaphore_wait(hello.at[step], 2)

    start_ships(0)
    keep(0)
    tell(0)
    mark_slots(EARLY, SLOTS)
    take_slots(EARLY, SLOTS)
    start_ships(1)
    for t in range(1, STAGES):
        keep(t)
    col_max[...] = jnp.full(col_max.shape, LOWEST, F32)
    answer[...] = jnp.full(answer.shape, LOWEST, F32)
    for t in range(STAGES):
        relay(t)
        end_ships(t)
        if t + 2 < STAGES:
            start_ships(t + 2)
        hear(t)
        if t + 1 < STAGES:
            tell(t + 1)
        if t == 0:
            everyone, place_in, _ = ranks(list(range(CLUSTERS)))
            own_rank = jnp.zeros((LINES, 128), F32)
            for number, mask in enumerate(everyone):
                own_rank = own_rank + mask * place_in[number * LINES : (number + 1) * LINES]
            rank_of[...] = own_rank

    for t in range(STAGES):
        swap(t).wait_recv()
    pair_own()
    for t in range(STAGES):
        await_near(t)
        pair_near(t)

    for group in (NEXT, PREVIOUS, OTHER, OWN):
        for t in range(STAGES):
            start = group * REGION + t * GROUP
            best = jnp.max(col_max[:, start : start + GROUP], axis=0, keepdims=True)
            answer[group, t : t + 1] = jnp.maximum(answer[group, t : t + 1], best)

    def give(group):
        device = {OTHER: sibling, NEXT: from_ahead, PREVIOUS: from_behind}[group]
        return pltpu.make_async_remote_copy(
            src_ref=answer.at[group], dst_ref=near.at[group], send_sem=near_sent.at[group],
            recv_sem=back_near.at[group], device_id=(device, z), device_id_type=MESH,
        )

    for group in (NEXT, PREVIOUS, OTHER):
        give(group).start()
    best = answer[OWN]
    for group in (OTHER, NEXT, PREVIOUS):
        arrival(near.at[group], back_near.at[group]).wait()
        best = jnp.maximum(best, near[group])
    block_of = lax.div(iota((8, 128), 1), PIECE)
    moved = {by: pltpu.roll(best, by * PIECE % 128, 1) for by in range(1 - SIDE, STAGES)}
    for source in range(SIDE):
        spaced = jnp.zeros((8, 128), F32)
        for t in range(STAGES):
            spaced = jnp.where((iota((8, 128), 0) == t) & (block_of == t), moved[t - source], spaced)
        final[source] = jnp.sum(spaced, axis=0, keepdims=True)

    number = SIDE * z + x

    def spread(step, up):
        column = lax.rem(x + step, SIDE)
        return pltpu.make_async_remote_copy(
            src_ref=final.at[column], dst_ref=returned.at[number], send_sem=back_sent.at[up, step],
            recv_sem=back_arrive, device_id=(place(column, y, core), plane(z + up)), device_id_type=MESH,
        )

    spreads = [spread(step, up) for up in (4, 3, 5, 2, 6, 1, 7, 0) for step in (2, 1, 3, 0) if step or up]
    for copy in spreads:
        copy.start()
    pltpu.make_async_copy(final.at[x], returned.at[number], back_arrive).start()
    pltpu.make_async_copy(returned, returned, back_arrive).wait()

    found = returned[...].reshape(CLUSTERS, 128)
    high = found.astype(BF16)
    rest = found - high.astype(F32)
    middle = rest.astype(BF16)
    low = (rest - middle.astype(F32)).astype(BF16)
    parts = jnp.concatenate([high, middle, low], axis=0)
    slot = iota((128, 128), 0).astype(F32)
    line = iota((CLUSTERS, 128), 0)
    for r in range(LINES):
        chosen = jnp.where(slot == rank_of[r : r + 1, :], 1.0, 0.0).astype(BF16)
        taken = jnp.dot(parts, chosen, preferred_element_type=F32)
        taken = taken[0:CLUSTERS] + taken[CLUSTERS : 2 * CLUSTERS] + taken[2 * CLUSTERS :]
        out_ref[r : r + 1] = jnp.sum(
            jnp.where(line == cluster_ref[r : r + 1, :], taken, 0.0), axis=0, keepdims=True
        )

    for group in (OTHER, NEXT, PREVIOUS):
        give(group).wait_send()
    for copy in spreads:
        copy.wait_send()

    def end_stage(t, carry):
        swap(t).wait_send()
        for source in range(SIDE):
            for group in (NEXT, PREVIOUS):
                pass_on(t, source, piece(t, OWN, source), group).wait_send()
        return carry

    lax.fori_loop(0, STAGES, end_stage, 0)


def local(embeds, cluster_of):
    dma = pltpu.SemaphoreType.DMA
    out = pl.pallas_call(
        kernel,
        out_shape=jax.ShapeDtypeStruct((LINES, 128), F32),
        in_specs=[pl.BlockSpec(memory_space=pltpu.VMEM), pl.BlockSpec(memory_space=pl.ANY)],
        out_specs=pl.BlockSpec(memory_space=pltpu.VMEM),
        scratch_shapes=[
            pltpu.VMEM((DOCS, WIDTH), BF16),
            pltpu.VMEM((4 * (SLOTS - EARLY), DOCS), BF16),
            pltpu.VMEM((4 * (SLOTS - EARLY), WIDTH), F32),
            pltpu.VMEM((4 * SLOTS, WIDTH), BF16),
            pltpu.VMEM((MEMBERS, WIDTH), BF16),
            pltpu.VMEM((8, MEMBERS), F32),
            pltpu.VMEM((REGION, 128), F32),
            pltpu.VMEM((8, MEMBERS), F32),
            pltpu.VMEM((4, 8, 128), F32),
            pltpu.VMEM((4, 8, 128), F32),
            pltpu.VMEM((SIDE, 1, 128), F32),
            pltpu.VMEM((CLUSTERS, 1, 128), F32),
            pltpu.VMEM((LINES, 128), F32),
            dma,
            dma((STAGES, SIDE)),
            dma((STAGES, SIDE)),
            dma((STAGES, SIDE, 2)),
            dma((STAGES, SIDE, 2)),
            dma((STAGES,)),
            dma((STAGES,)),
            dma((4,)),
            dma((4,)),
            dma((PLANES, SIDE)),
            dma,
            pltpu.SemaphoreType.REGULAR((STAGES,)),
        ],
        compiler_params=pltpu.CompilerParams(
            collective_id=0, has_side_effects=True, vmem_limit_bytes=48 * 2**20
        ),
        cost_estimate=pl.CostEstimate(flops=8 * 10**9, bytes_accessed=4 * 2**20, transcendentals=512),
    )(cluster_of.reshape(LINES, 128), embeds)
    return out.reshape(DOCS)


def solution(mesh):
    return jax.shard_map(
        local,
        mesh=mesh,
        in_specs=(P("docs", None), P("docs")),
        out_specs=P("docs"),
        check_vma=False,
    )
```

```python
import jax
import jax.numpy as jnp
from jax import lax
from jax.experimental import pallas as pl
from jax.experimental.pallas import tpu as pltpu
from jax.sharding import PartitionSpec as P


EPSILON = 1e-06
LOWEST = -3e38
FAR = -1e30
PADDED = 2.0

SIDE = 4
PLANES = 8
CLUSTERS = SIDE * PLANES
DOCS = 2048
WIDTH = 1024
SLOTS = 128
STAGES = 4
PIECE = SLOTS // STAGES
GROUP = SIDE * PIECE
REGION = STAGES * GROUP
MEMBERS = 4 * REGION
LOADS = 8
LINES = DOCS // 128
OWN, OTHER, PREVIOUS, NEXT = range(4)

MESH = pl.DeviceIdType.MESH
F32 = jnp.float32
BF16 = jnp.bfloat16
NT = (((1,), (1,)), ((), ()))


def iota(shape, axis):
    return lax.broadcasted_iota(jnp.int32, shape, axis)


def kernel(
    cluster_hbm, embeds_ref, out_ref,
    cluster_ref, rows, pick, gathered, blocks, members, col_bias, row_max, col_max, answer,
    near, final, returned, rank_of,
    cluster_sem, load_sem, shipped, arrive, passed, near_arrive, swap_sent, swap_arrive, near_sent, back_near, back_sent,
    back_arrive, hello,
):
    docs = lax.axis_index("docs")
    z = lax.axis_index("grp")
    core = lax.rem(docs, 2)
    x = lax.rem(lax.div(docs, 2), SIDE)
    y = lax.div(docs, 2 * SIDE)

    def place(px, py, pcore):
        return (lax.rem(py + SIDE, SIDE) * SIDE + lax.rem(px, SIDE)) * 2 + lax.rem(pcore, 2)

    def plane(pz):
        return lax.rem(pz + PLANES, PLANES)

    def turn(py):
        return lax.div(lax.rem(py + 3, SIDE), 2)

    sibling = place(x, y, core + 1)
    ahead = place(x, y + 1, core + turn(y + 1))
    behind = place(x, y - 1, core)
    from_ahead = place(x, y + 1, core)
    from_behind = place(x, y - 1, core + turn(y))

    cluster_load = pltpu.make_async_copy(cluster_hbm, cluster_ref, cluster_sem)
    cluster_load.start()
    loads = []
    for part in range(LOADS):
        span = pl.ds(part * (DOCS // LOADS), DOCS // LOADS)
        loads.append(pltpu.make_async_copy(embeds_ref.at[span], rows.at[span], load_sem.at[part]))
        loads[-1].start()

    barrier = pltpu.get_barrier_semaphore()

    def greet(device):
        pl.semaphore_signal(barrier, inc=1, device_id=device, device_id_type=MESH)

    for step in range(1, SIDE):
        greet((place(x + step, y, core), z))
    greet((from_ahead, z))
    greet((from_behind, z))
    greet((sibling, z))
    greet((docs, plane(z + 1)))
    greet((docs, plane(z - 1)))

    cluster_load.wait()
    clusters = cluster_ref[...]

    def ranks(numbers):
        member = [jnp.where(clusters == number, 1.0, 0.0).astype(F32) for number in numbers]
        stacked = jnp.concatenate(member, axis=0).astype(BF16)
        before = jnp.where(iota((128, 128), 0) < iota((128, 128), 1), 1.0, 0.0).astype(BF16)
        within = jnp.dot(stacked, before, preferred_element_type=F32)
        totals = jnp.dot(stacked, jnp.ones((128, 128), BF16), preferred_element_type=F32)
        lines = len(member) * LINES
        above = (iota((lines, lines), 1) < iota((lines, lines), 0)) & (
            lax.div(iota((lines, lines), 1), LINES) == lax.div(iota((lines, lines), 0), LINES)
        )
        offsets = jnp.dot(
            jnp.where(above, 1.0, 0.0).astype(BF16), totals.astype(BF16), preferred_element_type=F32
        )
        return member, within + offsets, totals

    member, rank, totals = ranks([SIDE * z + b for b in range(4)])
    positions = [jnp.where(member[b] > 0, rank[b * LINES : (b + 1) * LINES], -1.0) for b in range(4)]
    counts = [jnp.sum(totals[b * LINES : (b + 1) * LINES], axis=0, keepdims=True) for b in range(4)]

    def mark_slots(t):
        slot = iota((PIECE, 128), 0).astype(F32) + t * PIECE
        for b in range(4):
            for r in range(LINES):
                pick[b * PIECE : (b + 1) * PIECE, r * 128 : (r + 1) * 128] = jnp.where(
                    slot == positions[b][r : r + 1], 1.0, 0.0
                ).astype(BF16)

    def scale_slots(t):
        slot = iota((PIECE, 128), 0).astype(F32) + t * PIECE
        for b in range(4):
            values = gathered[b * PIECE : (b + 1) * PIECE, :]
            inverse = lax.rsqrt(jnp.sum(values * values, axis=1, keepdims=True) + EPSILON)
            scaled = values * inverse
            empty = (slot >= counts[b]) & (iota((PIECE, 128), 1) == 0)
            at = (t * 4 + b) * PIECE
            blocks[at : at + PIECE, :] = scaled.astype(BF16)
            blocks[at : at + PIECE, 0:128] = jnp.where(empty, PADDED, scaled[:, 0:128]).astype(BF16)

    def gather_part(part):
        span = slice(part * (DOCS // LOADS), (part + 1) * (DOCS // LOADS))
        for c in range(0, WIDTH, 256):
            taken = jnp.dot(pick[:, span], rows[span, c : c + 256], preferred_element_type=F32)
            gathered[:, c : c + 256] = taken if part == 0 else gathered[:, c : c + 256] + taken

    def gather_all():
        def gather(n, carry):
            cols = pl.ds(pl.multiple_of(n * 256, 256), 256)
            gathered[:, cols] = jnp.dot(pick[...], rows[:, cols], preferred_element_type=F32)
            return carry

        lax.fori_loop(0, WIDTH // 256, gather, 0)

    mark_slots(0)
    for part in range(LOADS):
        loads[part].wait()
        gather_part(part)
    scale_slots(0)
    pl.semaphore_wait(barrier, SIDE + 4)

    def piece(t, group, source):
        return members.at[pl.ds(pl.multiple_of(group * REGION + t * GROUP + source * PIECE, PIECE), PIECE)]

    def block(t, b):
        return blocks.at[pl.ds(pl.multiple_of((t * 4 + b) * PIECE, PIECE), PIECE)]

    def arrival(ref, sem):
        return pltpu.make_async_copy(ref, ref, sem)

    def ship(t, step):
        column = lax.rem(x + step, SIDE)
        return pltpu.make_async_remote_copy(
            src_ref=block(t, column), dst_ref=piece(t, OWN, x),
            send_sem=shipped.at[t, step], recv_sem=arrive.at[t, x],
            device_id=(place(column, y, core), z), device_id_type=MESH,
        )

    def pass_on(t, source, src, group):
        return pltpu.make_async_remote_copy(
            src_ref=src, dst_ref=piece(t, group, source),
            send_sem=passed.at[t, source, group - PREVIOUS], recv_sem=near_arrive.at[t, source, group - PREVIOUS],
            device_id=(behind if group == NEXT else ahead, z), device_id_type=MESH,
        )

    def pass_both(t, source, src):
        pass_on(t, source, src, NEXT).start()
        pass_on(t, source, src, PREVIOUS).start()

    def swap(t):
        return pltpu.make_async_remote_copy(
            src_ref=members.at[pl.ds(OWN * REGION + t * GROUP, GROUP)],
            dst_ref=members.at[pl.ds(OTHER * REGION + t * GROUP, GROUP)],
            send_sem=swap_sent.at[t], recv_sem=swap_arrive.at[t],
            device_id=(sibling, z), device_id_type=MESH,
        )

    def start_ships(t):
        for step in (2, 3, 1):
            ship(t, step).start()

    def end_ships(t):
        for step in (2, 3, 1):
            ship(t, step).wait_send()

    def keep(t):
        pass_both(t, x, block(t, x))
        pltpu.make_async_copy(block(t, x), piece(t, OWN, x), arrive.at[t, x]).start()

    def relay(t):
        for step in (3, 1, 2):
            source = lax.rem(x + step, SIDE)
            arrival(piece(t, OWN, source), arrive.at[t, source]).wait()
            pass_both(t, source, piece(t, OWN, source))
        arrival(piece(t, OWN, x), arrive.at[t, x]).wait()
        swap(t).start()

    def await_near(t):
        for source in range(SIDE):
            for group in (NEXT, PREVIOUS):
                arrival(piece(t, group, source), near_arrive.at[t, source, group - PREVIOUS]).wait()

    def tell(step):
        for way in (1, -1):
            pl.semaphore_signal(hello.at[step], inc=1, device_id=(docs, plane(z + way)), device_id_type=MESH)

    def mark(start, size):
        chosen = jnp.where((iota((16, 128), 0) < 8) & (iota((16, 128), 1) == 0), 1.0, 0.0).astype(BF16)
        heads = lax.dot_general(chosen, members[start : start + size, 0:128], NT, preferred_element_type=F32)
        col_bias[:, start : start + size] = jnp.where(heads[0:8] > 1.5, FAR, 0.0)

    def bias_of_rows(start, size):
        first = members[start : start + size, 0:128].astype(F32)[:, 0:1]
        return jnp.where(first > 1.5, FAR, 0.0)

    def scores(base, size, start, width):
        return lax.dot_general(
            members[base : base + size, :], members[start : start + width, :], NT, preferred_element_type=F32
        )

    def along_rows(best, score, start, width):
        biased = score + col_bias[0:1, start : start + width]
        for c in range(0, width, 128):
            best = jnp.maximum(best, biased[:, c : c + 128])
        return best

    def turned(best):
        return jnp.max(best.T, axis=0, keepdims=True)

    def pair_own():
        row_max[...] = jnp.full((REGION, 128), LOWEST, F32)
        for n in range(2 * REGION // 256):
            start = n * 256
            mark(start, 256)
            score = scores(0, REGION, start, 256)
            if start < REGION:
                score = jnp.where(iota((REGION, 256), 0) == iota((REGION, 256), 1) + start, LOWEST, score)
            row_max[...] = along_rows(row_max[...], score, start, 256)
        for t in range(STAGES):
            answer[OWN, t : t + 1] = turned(row_max[t * GROUP : (t + 1) * GROUP, :])

    def pair(base, start, stop):
        bias = bias_of_rows(base, GROUP)
        best = jnp.full((GROUP, 128), LOWEST, F32)
        while start < stop:
            width = min(512, stop - start)
            score = scores(base, GROUP, start, width)
            best = along_rows(best, score, start, width)
            biased = (score + bias).reshape(GROUP // 8, 8, width)
            span = slice(start, start + width)
            col_max[:, span] = jnp.maximum(col_max[:, span], jnp.max(biased, axis=0))
            start += width
        return turned(best)

    def pair_near(t):
        nexts, previous = NEXT * REGION + t * GROUP, PREVIOUS * REGION + t * GROUP
        mark(previous, GROUP)
        answer[NEXT, t : t + 1] = pair(nexts, 0, previous + GROUP)
        if t:
            answer[PREVIOUS, t : t + 1] = pair(previous, NEXT * REGION, nexts)
        if t + 1 < STAGES:
            mark(nexts, GROUP)

    def hear(step):
        pl.semaphore_wait(hello.at[step], 2)

    start_ships(0)
    keep(0)
    tell(0)
    for t in range(1, STAGES):
        mark_slots(t)
        gather_all()
        scale_slots(t)
        keep(t)
        if t == 1:
            start_ships(t)
    col_max[...] = jnp.full(col_max.shape, LOWEST, F32)
    answer[...] = jnp.full(answer.shape, LOWEST, F32)
    for t in range(STAGES):
        relay(t)
        end_ships(t)
        if t + 2 < STAGES:
            start_ships(t + 2)
        hear(t)
        if t + 1 < STAGES:
            tell(t + 1)
        if t == 0:
            everyone, place_in, _ = ranks(list(range(CLUSTERS)))
            own_rank = jnp.zeros((LINES, 128), F32)
            for number, mask in enumerate(everyone):
                own_rank = own_rank + mask * place_in[number * LINES : (number + 1) * LINES]
            rank_of[...] = own_rank

    for t in range(STAGES):
        swap(t).wait_recv()
    pair_own()
    for t in range(STAGES):
        await_near(t)
        pair_near(t)

    for group in (NEXT, PREVIOUS, OTHER, OWN):
        for t in range(STAGES):
            start = group * REGION + t * GROUP
            best = jnp.max(col_max[:, start : start + GROUP], axis=0, keepdims=True)
            answer[group, t : t + 1] = jnp.maximum(answer[group, t : t + 1], best)

    def give(group):
        device = {OTHER: sibling, NEXT: from_ahead, PREVIOUS: from_behind}[group]
        return pltpu.make_async_remote_copy(
            src_ref=answer.at[group], dst_ref=near.at[group], send_sem=near_sent.at[group],
            recv_sem=back_near.at[group], device_id=(device, z), device_id_type=MESH,
        )

    for group in (NEXT, PREVIOUS, OTHER):
        give(group).start()
    best = answer[OWN]
    for group in (OTHER, NEXT, PREVIOUS):
        arrival(near.at[group], back_near.at[group]).wait()
        best = jnp.maximum(best, near[group])
    block_of = lax.div(iota((8, 128), 1), PIECE)
    moved = {by: pltpu.roll(best, by * PIECE % 128, 1) for by in range(1 - SIDE, STAGES)}
    for source in range(SIDE):
        spaced = jnp.zeros((8, 128), F32)
        for t in range(STAGES):
            spaced = jnp.where((iota((8, 128), 0) == t) & (block_of == t), moved[t - source], spaced)
        final[source] = jnp.sum(spaced, axis=0, keepdims=True)

    number = SIDE * z + x

    def spread(step, up):
        column = lax.rem(x + step, SIDE)
        return pltpu.make_async_remote_copy(
            src_ref=final.at[column], dst_ref=returned.at[number], send_sem=back_sent.at[up, step],
            recv_sem=back_arrive, device_id=(place(column, y, core), plane(z + up)), device_id_type=MESH,
        )

    spreads = [spread(step, up) for up in (4, 3, 5, 2, 6, 1, 7, 0) for step in (2, 1, 3, 0) if step or up]
    for copy in spreads:
        copy.start()
    pltpu.make_async_copy(final.at[x], returned.at[number], back_arrive).start()

    for group in (OTHER, NEXT, PREVIOUS):
        give(group).wait_send()

    def end_stage(t, carry):
        swap(t).wait_send()
        for source in range(SIDE):
            for group in (NEXT, PREVIOUS):
                pass_on(t, source, piece(t, OWN, source), group).wait_send()
        return carry

    lax.fori_loop(0, STAGES, end_stage, 0)
    for copy in spreads:
        copy.wait_send()
    pltpu.make_async_copy(returned, returned, back_arrive).wait()

    found = returned[...].reshape(CLUSTERS, 128)
    high = found.astype(BF16)
    rest = found - high.astype(F32)
    middle = rest.astype(BF16)
    low = (rest - middle.astype(F32)).astype(BF16)
    parts = jnp.concatenate([high, middle, low], axis=0)
    slot = iota((128, 128), 0).astype(F32)
    line = iota((CLUSTERS, 128), 0)
    for r in range(LINES):
        chosen = jnp.where(slot == rank_of[r : r + 1, :], 1.0, 0.0).astype(BF16)
        taken = jnp.dot(parts, chosen, preferred_element_type=F32)
        taken = taken[0:CLUSTERS] + taken[CLUSTERS : 2 * CLUSTERS] + taken[2 * CLUSTERS :]
        out_ref[r : r + 1] = jnp.sum(
            jnp.where(line == cluster_ref[r : r + 1, :], taken, 0.0), axis=0, keepdims=True
        )


def local(embeds, cluster_of):
    dma = pltpu.SemaphoreType.DMA
    out = pl.pallas_call(
        kernel,
        out_shape=jax.ShapeDtypeStruct((LINES, 128), F32),
        in_specs=[pl.BlockSpec(memory_space=pl.ANY)] * 2,
        out_specs=pl.BlockSpec(memory_space=pltpu.VMEM),
        scratch_shapes=[
            pltpu.VMEM((LINES, 128), jnp.int32),
            pltpu.VMEM((DOCS, WIDTH), BF16),
            pltpu.VMEM((GROUP, DOCS), BF16),
            pltpu.VMEM((GROUP, WIDTH), F32),
            pltpu.VMEM((4 * SLOTS, WIDTH), BF16),
            pltpu.VMEM((MEMBERS, WIDTH), BF16),
            pltpu.VMEM((8, MEMBERS), F32),
            pltpu.VMEM((REGION, 128), F32),
            pltpu.VMEM((8, MEMBERS), F32),
            pltpu.VMEM((4, 8, 128), F32),
            pltpu.VMEM((4, 8, 128), F32),
            pltpu.VMEM((SIDE, 1, 128), F32),
            pltpu.VMEM((CLUSTERS, 1, 128), F32),
            pltpu.VMEM((LINES, 128), F32),
            dma,
            dma((LOADS,)),
            dma((STAGES, SIDE)),
            dma((STAGES, SIDE)),
            dma((STAGES, SIDE, 2)),
            dma((STAGES, SIDE, 2)),
            dma((STAGES,)),
            dma((STAGES,)),
            dma((4,)),
            dma((4,)),
            dma((PLANES, SIDE)),
            dma,
            pltpu.SemaphoreType.REGULAR((STAGES,)),
        ],
        compiler_params=pltpu.CompilerParams(
            collective_id=0, has_side_effects=True, vmem_limit_bytes=53 * 2**20
        ),
        cost_estimate=pl.CostEstimate(flops=8 * 10**9, bytes_accessed=4 * 2**20, transcendentals=512),
    )(cluster_of.reshape(LINES, 128), embeds)
    return out.reshape(DOCS)


def solution(mesh):
    return jax.shard_map(
        local,
        mesh=mesh,
        in_specs=(P("docs", None), P("docs")),
        out_specs=P("docs"),
        check_vma=False,
    )
```

```python
import jax
import jax.numpy as jnp
from jax import lax
from jax.experimental import pallas as pl
from jax.experimental.pallas import tpu as pltpu
from jax.sharding import PartitionSpec as P


EPSILON = 1e-06
LOWEST = -3e38
FAR = -1e30
PADDED = 2.0

SIDE = 4
PLANES = 8
CLUSTERS = SIDE * PLANES
DOCS = 2048
WIDTH = 1024
SLOTS = 128
STAGES = 4
PIECE = SLOTS // STAGES
GROUP = SIDE * PIECE
REGION = STAGES * GROUP
MEMBERS = 4 * REGION
LOADS = 8
DETOURS = (0, 1)
FAR_SOURCE = 3
LINES = DOCS // 128
OWN, OTHER, Y_PART, X_PART = range(4)

MESH = pl.DeviceIdType.MESH
F32 = jnp.float32
BF16 = jnp.bfloat16
NT = (((1,), (1,)), ((), ()))


def iota(shape, axis):
    return lax.broadcasted_iota(jnp.int32, shape, axis)


def kernel(
    cluster_hbm, embeds_ref, out_ref,
    cluster_ref, rows, pick, gathered, blocks, members, col_bias, row_max, col_max, answer,
    near, final, returned, rank_of, detours,
    cluster_sem, load_sem, shipped, arrive, passed, near_arrive, swap_sent, swap_arrive, near_sent, back_near, back_sent,
    back_arrive, hello, detour_sent, detour_arrive, detour_passed,
):
    docs = lax.axis_index("docs")
    z = lax.axis_index("grp")
    core = lax.rem(docs, 2)
    x = lax.rem(lax.div(docs, 2), SIDE)
    y = lax.div(docs, 2 * SIDE)

    def place(px, py, pcore):
        return (lax.rem(py + SIDE, SIDE) * SIDE + lax.rem(px + SIDE, SIDE)) * 2 + lax.rem(pcore, 2)

    def plane(pz):
        return lax.rem(pz + PLANES, PLANES)

    shifted = lax.rem(z, 2)
    odd_x = lax.rem(x + shifted, 2)
    odd_y = lax.rem(y + shifted, 2)
    in_x, out_x = x + 1 - 2 * odd_x, x - 1 + 2 * odd_x
    in_y, out_y = y + 1 - 2 * odd_y, y - 1 + 2 * odd_y

    def cluster_at(px, py):
        tile_x = lax.div(lax.rem(px + SIDE - shifted, SIDE), 2)
        tile_y = lax.div(lax.rem(py + SIDE - shifted, SIDE), 2)
        return SIDE * z + 2 * tile_y + tile_x

    chips = [(x, y), (out_x, y), (x, out_y), (out_x, out_y)]
    numbers = [cluster_at(px + SIDE, py + SIDE) for px, py in chips]

    sibling = place(x, y, core + 1)
    to_x = place(in_x, y, core)
    to_y = place(x, in_y, core + 1 - odd_y)
    from_y = place(x, in_y, core + odd_y)

    cluster_load = pltpu.make_async_copy(cluster_hbm, cluster_ref, cluster_sem)
    cluster_load.start()
    loads = []
    for part in range(LOADS):
        span = pl.ds(part * (DOCS // LOADS), DOCS // LOADS)
        loads.append(pltpu.make_async_copy(embeds_ref.at[span], rows.at[span], load_sem.at[part]))
        loads[-1].start()

    barrier = pltpu.get_barrier_semaphore()

    def greet(device):
        pl.semaphore_signal(barrier, inc=1, device_id=device, device_id_type=MESH)

    for dx in (-1, 0, 1):
        for dy in (-1, 0, 1):
            if dx or dy:
                greet((place(x + dx, y + dy, core), z))
    greet((place(x, y + 1, core + 1), z))
    greet((place(x, y - 1, core + 1), z))
    greet((sibling, z))
    greet((docs, plane(z + 1)))
    greet((docs, plane(z - 1)))
    greet((place(out_x, y, core), plane(z - 1)))
    greet((place(x, out_y, core + 1 - odd_y), plane(z + 1)))

    cluster_load.wait()
    clusters = cluster_ref[...]

    def ranks(numbers):
        member = [jnp.where(clusters == number, 1.0, 0.0).astype(F32) for number in numbers]
        stacked = jnp.concatenate(member, axis=0).astype(BF16)
        before = jnp.where(iota((128, 128), 0) < iota((128, 128), 1), 1.0, 0.0).astype(BF16)
        within = jnp.dot(stacked, before, preferred_element_type=F32)
        totals = jnp.dot(stacked, jnp.ones((128, 128), BF16), preferred_element_type=F32)
        lines = len(member) * LINES
        above = (iota((lines, lines), 1) < iota((lines, lines), 0)) & (
            lax.div(iota((lines, lines), 1), LINES) == lax.div(iota((lines, lines), 0), LINES)
        )
        offsets = jnp.dot(
            jnp.where(above, 1.0, 0.0).astype(BF16), totals.astype(BF16), preferred_element_type=F32
        )
        return member, within + offsets, totals

    member, rank, totals = ranks(numbers)
    positions = [jnp.where(member[b] > 0, rank[b * LINES : (b + 1) * LINES], -1.0) for b in range(4)]
    counts = [jnp.sum(totals[b * LINES : (b + 1) * LINES], axis=0, keepdims=True) for b in range(4)]

    def mark_slots(t):
        slot = iota((PIECE, 128), 0).astype(F32) + t * PIECE
        for b in range(4):
            for r in range(LINES):
                pick[b * PIECE : (b + 1) * PIECE, r * 128 : (r + 1) * 128] = jnp.where(
                    slot == positions[b][r : r + 1], 1.0, 0.0
                ).astype(BF16)

    def scale_slots(t):
        slot = iota((PIECE, 128), 0).astype(F32) + t * PIECE
        for b in range(4):
            values = gathered[b * PIECE : (b + 1) * PIECE, :]
            inverse = lax.rsqrt(jnp.sum(values * values, axis=1, keepdims=True) + EPSILON)
            scaled = values * inverse
            empty = (slot >= counts[b]) & (iota((PIECE, 128), 1) == 0)
            at = (t * 4 + b) * PIECE
            blocks[at : at + PIECE, :] = scaled.astype(BF16)
            blocks[at : at + PIECE, 0:128] = jnp.where(empty, PADDED, scaled[:, 0:128]).astype(BF16)

    def gather_part(part):
        span = slice(part * (DOCS // LOADS), (part + 1) * (DOCS // LOADS))
        for c in range(0, WIDTH, 256):
            taken = jnp.dot(pick[:, span], rows[span, c : c + 256], preferred_element_type=F32)
            gathered[:, c : c + 256] = taken if part == 0 else gathered[:, c : c + 256] + taken

    def gather_all():
        def gather(n, carry):
            cols = pl.ds(pl.multiple_of(n * 256, 256), 256)
            gathered[:, cols] = jnp.dot(pick[...], rows[:, cols], preferred_element_type=F32)
            return carry

        lax.fori_loop(0, WIDTH // 256, gather, 0)

    mark_slots(0)
    for part in range(LOADS):
        loads[part].wait()
        gather_part(part)
    scale_slots(0)
    pl.semaphore_wait(barrier, 15)

    def piece(t, group, source):
        return members.at[pl.ds(pl.multiple_of(group * REGION + t * GROUP + source * PIECE, PIECE), PIECE)]

    def block(t, b):
        return blocks.at[pl.ds(pl.multiple_of((t * 4 + b) * PIECE, PIECE), PIECE)]

    def arrival(ref, sem):
        return pltpu.make_async_copy(ref, ref, sem)

    def ship(t, b):
        return pltpu.make_async_remote_copy(
            src_ref=block(t, b), dst_ref=piece(t, OWN, b), send_sem=shipped.at[t, b], recv_sem=arrive.at[t, b],
            device_id=(place(*chips[b], core), z), device_id_type=MESH,
        )

    def pass_on(t, source, src, group):
        return pltpu.make_async_remote_copy(
            src_ref=src, dst_ref=piece(t, group, source),
            send_sem=passed.at[t, source, group - Y_PART], recv_sem=near_arrive.at[t, source, group - Y_PART],
            device_id=(to_x if group == X_PART else to_y, z), device_id_type=MESH,
        )

    def pass_both(t, source, src):
        pass_on(t, source, src, X_PART).start()
        pass_on(t, source, src, Y_PART).start()

    def detour(t, group):
        way = group - Y_PART
        return pltpu.make_async_remote_copy(
            src_ref=piece(t, OWN, FAR_SOURCE), dst_ref=detours.at[way, t],
            send_sem=detour_sent.at[way, t], recv_sem=detour_arrive.at[way, t],
            device_id=(to_x, plane(z + 1)) if group == X_PART else (to_y, plane(z - 1)), device_id_type=MESH,
        )

    def pass_detour(t, group):
        way = group - Y_PART
        return pltpu.make_async_remote_copy(
            src_ref=detours.at[way, t], dst_ref=piece(t, group, FAR_SOURCE),
            send_sem=detour_passed.at[way, t], recv_sem=near_arrive.at[t, FAR_SOURCE, way],
            device_id=(docs, plane(z - 1) if group == X_PART else plane(z + 1)), device_id_type=MESH,
        )

    def pass_detours(t):
        for group in (X_PART, Y_PART):
            way = group - Y_PART
            arrival(detours.at[way, t], detour_arrive.at[way, t]).wait()
            pass_detour(t, group).start()

    def swap(t):
        return pltpu.make_async_remote_copy(
            src_ref=members.at[pl.ds(OWN * REGION + t * GROUP, GROUP)],
            dst_ref=members.at[pl.ds(OTHER * REGION + t * GROUP, GROUP)],
            send_sem=swap_sent.at[t], recv_sem=swap_arrive.at[t],
            device_id=(sibling, z), device_id_type=MESH,
        )

    def start_ships(t):
        for b in (3, 1, 2):
            ship(t, b).start()

    def end_ships(t):
        for b in (3, 1, 2):
            ship(t, b).wait_send()

    def keep(t):
        pass_both(t, 0, block(t, 0))
        pltpu.make_async_copy(block(t, 0), piece(t, OWN, 0), arrive.at[t, 0]).start()

    def relay(t):
        for source in (1, 2, 3):
            arrival(piece(t, OWN, source), arrive.at[t, source]).wait()
            if source == FAR_SOURCE and t in DETOURS:
                detour(t, X_PART).start()
                detour(t, Y_PART).start()
            else:
                pass_both(t, source, piece(t, OWN, source))
        arrival(piece(t, OWN, 0), arrive.at[t, 0]).wait()
        swap(t).start()

    def await_near(t):
        for source in range(SIDE):
            for group in (X_PART, Y_PART):
                arrival(piece(t, group, source), near_arrive.at[t, source, group - Y_PART]).wait()

    def tell(step):
        for way in (1, -1):
            pl.semaphore_signal(hello.at[step], inc=1, device_id=(docs, plane(z + way)), device_id_type=MESH)

    def mark(start, size):
        chosen = jnp.where((iota((16, 128), 0) < 8) & (iota((16, 128), 1) == 0), 1.0, 0.0).astype(BF16)
        heads = lax.dot_general(chosen, members[start : start + size, 0:128], NT, preferred_element_type=F32)
        col_bias[:, start : start + size] = jnp.where(heads[0:8] > 1.5, FAR, 0.0)

    def bias_of_rows(start, size):
        first = members[start : start + size, 0:128].astype(F32)[:, 0:1]
        return jnp.where(first > 1.5, FAR, 0.0)

    def scores(base, size, start, width):
        return lax.dot_general(
            members[base : base + size, :], members[start : start + width, :], NT, preferred_element_type=F32
        )

    def along_rows(best, score, start, width):
        biased = score + col_bias[0:1, start : start + width]
        for c in range(0, width, 128):
            best = jnp.maximum(best, biased[:, c : c + 128])
        return best

    def turned(best):
        return jnp.max(best.T, axis=0, keepdims=True)

    def pair_own():
        row_max[...] = jnp.full((REGION, 128), LOWEST, F32)
        for n in range(2 * REGION // 256):
            start = n * 256
            mark(start, 256)
            score = scores(0, REGION, start, 256)
            if start < REGION:
                score = jnp.where(iota((REGION, 256), 0) == iota((REGION, 256), 1) + start, LOWEST, score)
            row_max[...] = along_rows(row_max[...], score, start, 256)
        for t in range(STAGES):
            answer[OWN, t : t + 1] = turned(row_max[t * GROUP : (t + 1) * GROUP, :])

    def pair(base, spans):
        bias = bias_of_rows(base, GROUP)
        best = jnp.full((GROUP, 128), LOWEST, F32)
        for start, width in spans:
            span = pl.ds(start, width)
            score = lax.dot_general(
                members[base : base + GROUP, :], members[span, :], NT, preferred_element_type=F32
            )
            biased = score + col_bias[0:1, span]
            for c in range(0, width, 128):
                best = jnp.maximum(best, biased[:, c : c + 128])
            biased = (score + bias).reshape(GROUP // 8, 8, width)
            col_max[:, span] = jnp.maximum(col_max[:, span], jnp.max(biased, axis=0))
        return turned(best)

    facing = pl.multiple_of(odd_x * REGION, REGION)

    def pair_near(t):
        to_pair_x, to_pair_y = X_PART * REGION + t * GROUP, Y_PART * REGION + t * GROUP
        mark(to_pair_y, GROUP)
        answer[X_PART, t : t + 1] = pair(to_pair_x, [(facing, REGION), (Y_PART * REGION, (t + 1) * GROUP)])
        spans = [(OWN * REGION, REGION)]
        if t:
            spans.append((X_PART * REGION, t * GROUP))
        answer[Y_PART, t : t + 1] = pair(to_pair_y, spans)
        if t + 1 < STAGES:
            mark(to_pair_x, GROUP)

    def hear(step):
        pl.semaphore_wait(hello.at[step], 2)

    start_ships(0)
    keep(0)
    tell(0)
    for t in range(1, STAGES):
        mark_slots(t)
        gather_all()
        scale_slots(t)
        if t in (1, 3):
            start_ships((t + 1) // 2)
        keep(t)
    col_max[...] = jnp.full(col_max.shape, LOWEST, F32)
    answer[...] = jnp.full(answer.shape, LOWEST, F32)
    for t in range(STAGES):
        relay(t)
        if t == 1:
            start_ships(3)
        if t - 1 in DETOURS:
            pass_detours(t - 1)
        hear(t)
        if t + 1 < STAGES:
            tell(t + 1)
        if t == 0:
            everyone, place_in, _ = ranks(list(range(CLUSTERS)))
            own_rank = jnp.zeros((LINES, 128), F32)
            for number, mask in enumerate(everyone):
                own_rank = own_rank + mask * place_in[number * LINES : (number + 1) * LINES]
            rank_of[...] = own_rank

    for t in range(STAGES):
        swap(t).wait_recv()
    pair_own()
    for t in range(STAGES):
        await_near(t)
        pair_near(t)

    for group in (X_PART, Y_PART, OTHER, OWN):
        for t in range(STAGES):
            start = group * REGION + t * GROUP
            best = jnp.max(col_max[:, start : start + GROUP], axis=0, keepdims=True)
            answer[group, t : t + 1] = jnp.maximum(answer[group, t : t + 1], best)

    def give(group):
        device = {OTHER: sibling, X_PART: to_x, Y_PART: from_y}[group]
        return pltpu.make_async_remote_copy(
            src_ref=answer.at[group], dst_ref=near.at[group], send_sem=near_sent.at[group],
            recv_sem=back_near.at[group], device_id=(device, z), device_id_type=MESH,
        )

    for group in (X_PART, Y_PART, OTHER):
        give(group).start()
    best = answer[OWN]
    for group in (OTHER, X_PART, Y_PART):
        arrival(near.at[group], back_near.at[group]).wait()
        best = jnp.maximum(best, near[group])
    block_of = lax.div(iota((8, 128), 1), PIECE)
    moved = {by: pltpu.roll(best, by * PIECE % 128, 1) for by in range(1 - SIDE, STAGES)}
    for source in range(SIDE):
        spaced = jnp.zeros((8, 128), F32)
        for t in range(STAGES):
            spaced = jnp.where((iota((8, 128), 0) == t) & (block_of == t), moved[t - source], spaced)
        final[source] = jnp.sum(spaced, axis=0, keepdims=True)

    def spread(source, up):
        return pltpu.make_async_remote_copy(
            src_ref=final.at[source], dst_ref=returned.at[numbers[0]], send_sem=back_sent.at[up, source],
            recv_sem=back_arrive, device_id=(place(*chips[source], core), plane(z + up)), device_id_type=MESH,
        )

    spreads = [spread(source, up) for up in (4, 3, 5, 2, 6, 1, 7, 0) for source in (3, 1, 2, 0) if source or up]
    for copy in spreads:
        copy.start()
    pltpu.make_async_copy(final.at[0], returned.at[numbers[0]], back_arrive).start()

    for group in (OTHER, X_PART, Y_PART):
        give(group).wait_send()

    for t in range(STAGES):
        end_ships(t)
        swap(t).wait_send()
        for group in (X_PART, Y_PART):
            for source in range(SIDE):
                if source != FAR_SOURCE or t not in DETOURS:
                    pass_on(t, source, piece(t, OWN, source), group).wait_send()
            if t in DETOURS:
                detour(t, group).wait_send()
                pass_detour(t, group).wait_send()
    for copy in spreads:
        copy.wait_send()
    pltpu.make_async_copy(returned, returned, back_arrive).wait()

    found = returned[...].reshape(CLUSTERS, 128)
    high = found.astype(BF16)
    rest = found - high.astype(F32)
    middle = rest.astype(BF16)
    low = (rest - middle.astype(F32)).astype(BF16)
    parts = jnp.concatenate([high, middle, low], axis=0)
    slot = iota((128, 128), 0).astype(F32)
    line = iota((CLUSTERS, 128), 0)
    for r in range(LINES):
        chosen = jnp.where(slot == rank_of[r : r + 1, :], 1.0, 0.0).astype(BF16)
        taken = jnp.dot(parts, chosen, preferred_element_type=F32)
        taken = taken[0:CLUSTERS] + taken[CLUSTERS : 2 * CLUSTERS] + taken[2 * CLUSTERS :]
        out_ref[r : r + 1] = jnp.sum(
            jnp.where(line == cluster_ref[r : r + 1, :], taken, 0.0), axis=0, keepdims=True
        )


def local(embeds, cluster_of):
    dma = pltpu.SemaphoreType.DMA
    out = pl.pallas_call(
        kernel,
        out_shape=jax.ShapeDtypeStruct((LINES, 128), F32),
        in_specs=[pl.BlockSpec(memory_space=pl.ANY)] * 2,
        out_specs=pl.BlockSpec(memory_space=pltpu.VMEM),
        scratch_shapes=[
            pltpu.VMEM((LINES, 128), jnp.int32),
            pltpu.VMEM((DOCS, WIDTH), BF16),
            pltpu.VMEM((GROUP, DOCS), BF16),
            pltpu.VMEM((GROUP, WIDTH), F32),
            pltpu.VMEM((4 * SLOTS, WIDTH), BF16),
            pltpu.VMEM((MEMBERS, WIDTH), BF16),
            pltpu.VMEM((8, MEMBERS), F32),
            pltpu.VMEM((REGION, 128), F32),
            pltpu.VMEM((8, MEMBERS), F32),
            pltpu.VMEM((4, 8, 128), F32),
            pltpu.VMEM((4, 8, 128), F32),
            pltpu.VMEM((SIDE, 1, 128), F32),
            pltpu.VMEM((CLUSTERS, 1, 128), F32),
            pltpu.VMEM((LINES, 128), F32),
            pltpu.VMEM((2, STAGES, PIECE, WIDTH), BF16),
            dma,
            dma((LOADS,)),
            dma((STAGES, SIDE)),
            dma((STAGES, SIDE)),
            dma((STAGES, SIDE, 2)),
            dma((STAGES, SIDE, 2)),
            dma((STAGES,)),
            dma((STAGES,)),
            dma((4,)),
            dma((4,)),
            dma((PLANES, SIDE)),
            dma,
            pltpu.SemaphoreType.REGULAR((STAGES,)),
            dma((2, STAGES)),
            dma((2, STAGES)),
            dma((2, STAGES)),
        ],
        compiler_params=pltpu.CompilerParams(
            collective_id=0, has_side_effects=True, vmem_limit_bytes=53 * 2**20
        ),
        cost_estimate=pl.CostEstimate(flops=8 * 10**9, bytes_accessed=4 * 2**20, transcendentals=512),
    )(cluster_of.reshape(LINES, 128), embeds)
    return out.reshape(DOCS)


def solution(mesh):
    return jax.shard_map(
        local,
        mesh=mesh,
        in_specs=(P("docs", None), P("docs")),
        out_specs=P("docs"),
        check_vma=False,
    )
```

```python
import jax
import jax.numpy as jnp
from jax import lax
from jax.experimental import pallas as pl
from jax.experimental.pallas import tpu as pltpu
from jax.sharding import PartitionSpec as P


EPSILON = 1e-06
LOWEST = -3e38
FAR = -1e30
PADDED = 2.0

SIDE = 4
PLANES = 8
CLUSTERS = SIDE * PLANES
DOCS = 2048
WIDTH = 1024
SLOTS = 128
STAGES = 4
PIECE = SLOTS // STAGES
GROUP = SIDE * PIECE
REGION = STAGES * GROUP
MEMBERS = 4 * REGION
LOADS = 8
DETOURS = ((0, 3), (1, 3))
LINES = DOCS // 128
OWN, OTHER, Y_PART, X_PART = range(4)

MESH = pl.DeviceIdType.MESH
F32 = jnp.float32
BF16 = jnp.bfloat16
NT = (((1,), (1,)), ((), ()))


def iota(shape, axis):
    return lax.broadcasted_iota(jnp.int32, shape, axis)


def kernel(
    cluster_hbm, embeds_ref, out_ref,
    cluster_ref, rows, pick, gathered, blocks, members, col_bias, row_max, col_max, answer,
    near, final, returned, rank_of, detours,
    cluster_sem, load_sem, shipped, arrive, passed, near_arrive, swap_sent, swap_arrive, near_sent, back_near, back_sent,
    back_arrive, hello, detour_sent, detour_arrive, detour_passed,
):
    docs = lax.axis_index("docs")
    z = lax.axis_index("grp")
    core = lax.rem(docs, 2)
    x = lax.rem(lax.div(docs, 2), SIDE)
    y = lax.div(docs, 2 * SIDE)

    def place(px, py, pcore):
        return (lax.rem(py + SIDE, SIDE) * SIDE + lax.rem(px + SIDE, SIDE)) * 2 + lax.rem(pcore, 2)

    def plane(pz):
        return lax.rem(pz + PLANES, PLANES)

    shifted = lax.rem(z, 2)
    odd_x = lax.rem(x + shifted, 2)
    odd_y = lax.rem(y + shifted, 2)
    in_x, out_x = x + 1 - 2 * odd_x, x - 1 + 2 * odd_x
    in_y, out_y = y + 1 - 2 * odd_y, y - 1 + 2 * odd_y

    def cluster_at(px, py):
        tile_x = lax.div(lax.rem(px + SIDE - shifted, SIDE), 2)
        tile_y = lax.div(lax.rem(py + SIDE - shifted, SIDE), 2)
        return SIDE * z + 2 * tile_y + tile_x

    chips = [(x, y), (out_x, y), (x, out_y), (out_x, out_y)]
    numbers = [cluster_at(px + SIDE, py + SIDE) for px, py in chips]

    sibling = place(x, y, core + 1)
    to_x = place(in_x, y, core)
    to_y = place(x, in_y, core + 1 - odd_y)
    from_y = place(x, in_y, core + odd_y)

    cluster_load = pltpu.make_async_copy(cluster_hbm, cluster_ref, cluster_sem)
    cluster_load.start()
    loads = []
    for part in range(LOADS):
        span = pl.ds(part * (DOCS // LOADS), DOCS // LOADS)
        loads.append(pltpu.make_async_copy(embeds_ref.at[span], rows.at[span], load_sem.at[part]))
        loads[-1].start()

    barrier = pltpu.get_barrier_semaphore()

    def greet(device):
        pl.semaphore_signal(barrier, inc=1, device_id=device, device_id_type=MESH)

    greet((place(out_x, y, core), plane(z - 1)))
    greet((place(x, out_y, core + 1 - odd_y), plane(z + 1)))
    for dx in (-1, 0, 1):
        for dy in (-1, 0, 1):
            if dx or dy:
                greet((place(x + dx, y + dy, core), z))
    greet((place(x, y + 1, core + 1), z))
    greet((place(x, y - 1, core + 1), z))
    greet((sibling, z))
    greet((docs, plane(z + 1)))
    greet((docs, plane(z - 1)))

    cluster_load.wait()
    clusters = cluster_ref[...]

    def ranks(numbers):
        member = [jnp.where(clusters == number, 1.0, 0.0).astype(F32) for number in numbers]
        stacked = jnp.concatenate(member, axis=0).astype(BF16)
        before = jnp.where(iota((128, 128), 0) < iota((128, 128), 1), 1.0, 0.0).astype(BF16)
        within = jnp.dot(stacked, before, preferred_element_type=F32)
        totals = jnp.dot(stacked, jnp.ones((128, 128), BF16), preferred_element_type=F32)
        lines = len(member) * LINES
        above = (iota((lines, lines), 1) < iota((lines, lines), 0)) & (
            lax.div(iota((lines, lines), 1), LINES) == lax.div(iota((lines, lines), 0), LINES)
        )
        offsets = jnp.dot(
            jnp.where(above, 1.0, 0.0).astype(BF16), totals.astype(BF16), preferred_element_type=F32
        )
        return member, within + offsets, totals

    member, rank, totals = ranks(numbers)
    positions = [jnp.where(member[b] > 0, rank[b * LINES : (b + 1) * LINES], -1.0) for b in range(4)]
    counts = [jnp.sum(totals[b * LINES : (b + 1) * LINES], axis=0, keepdims=True) for b in range(4)]

    def mark_slots(t):
        slot = iota((PIECE, 128), 0).astype(F32) + t * PIECE
        for b in range(4):
            for r in range(LINES):
                pick[b * PIECE : (b + 1) * PIECE, r * 128 : (r + 1) * 128] = jnp.where(
                    slot == positions[b][r : r + 1], 1.0, 0.0
                ).astype(BF16)

    def scale_slots(t):
        slot = iota((PIECE, 128), 0).astype(F32) + t * PIECE
        for b in range(4):
            values = gathered[b * PIECE : (b + 1) * PIECE, :]
            inverse = lax.rsqrt(jnp.sum(values * values, axis=1, keepdims=True) + EPSILON)
            scaled = values * inverse
            empty = (slot >= counts[b]) & (iota((PIECE, 128), 1) == 0)
            at = (t * 4 + b) * PIECE
            blocks[at : at + PIECE, :] = scaled.astype(BF16)
            blocks[at : at + PIECE, 0:128] = jnp.where(empty, PADDED, scaled[:, 0:128]).astype(BF16)

    def gather_part(part):
        span = slice(part * (DOCS // LOADS), (part + 1) * (DOCS // LOADS))
        for c in range(0, WIDTH, 256):
            taken = jnp.dot(pick[:, span], rows[span, c : c + 256], preferred_element_type=F32)
            gathered[:, c : c + 256] = taken if part == 0 else gathered[:, c : c + 256] + taken

    def gather_all():
        def gather(n, carry):
            cols = pl.ds(pl.multiple_of(n * 256, 256), 256)
            gathered[:, cols] = jnp.dot(pick[...], rows[:, cols], preferred_element_type=F32)
            return carry

        lax.fori_loop(0, WIDTH // 256, gather, 0)

    mark_slots(0)
    for part in range(LOADS):
        loads[part].wait()
        gather_part(part)
    scale_slots(0)
    pl.semaphore_wait(barrier, 15)

    def piece(t, group, source):
        return members.at[pl.ds(pl.multiple_of(group * REGION + t * GROUP + source * PIECE, PIECE), PIECE)]

    def block(t, b):
        return blocks.at[pl.ds(pl.multiple_of((t * 4 + b) * PIECE, PIECE), PIECE)]

    def arrival(ref, sem):
        return pltpu.make_async_copy(ref, ref, sem)

    def ship(t, b):
        return pltpu.make_async_remote_copy(
            src_ref=block(t, b), dst_ref=piece(t, OWN, b), send_sem=shipped.at[t, b], recv_sem=arrive.at[t, b],
            device_id=(place(*chips[b], core), z), device_id_type=MESH,
        )

    def pass_on(t, source, src, group):
        return pltpu.make_async_remote_copy(
            src_ref=src, dst_ref=piece(t, group, source),
            send_sem=passed.at[t, source, group - Y_PART], recv_sem=near_arrive.at[t, source, group - Y_PART],
            device_id=(to_x if group == X_PART else to_y, z), device_id_type=MESH,
        )

    def pass_both(t, source, src):
        pass_on(t, source, src, X_PART).start()
        pass_on(t, source, src, Y_PART).start()

    def detour(number, group):
        (t, source), way = DETOURS[number], group - Y_PART
        return pltpu.make_async_remote_copy(
            src_ref=piece(t, OWN, source), dst_ref=detours.at[way, number],
            send_sem=detour_sent.at[way, number], recv_sem=detour_arrive.at[way, number],
            device_id=(to_x, plane(z + 1)) if group == X_PART else (to_y, plane(z - 1)), device_id_type=MESH,
        )

    def pass_detour(number, group):
        (t, source), way = DETOURS[number], group - Y_PART
        return pltpu.make_async_remote_copy(
            src_ref=detours.at[way, number], dst_ref=piece(t, group, source),
            send_sem=detour_passed.at[way, number], recv_sem=near_arrive.at[t, source, way],
            device_id=(docs, plane(z - 1) if group == X_PART else plane(z + 1)), device_id_type=MESH,
        )

    def start_detours(t):
        for number, (stage, source) in enumerate(DETOURS):
            if stage == t:
                detour(number, X_PART).start()
                detour(number, Y_PART).start()

    def pass_detours(t):
        for number, (stage, source) in enumerate(DETOURS):
            if t == min(stage + 2, STAGES - 1):
                for group in (X_PART, Y_PART):
                    way = group - Y_PART
                    arrival(detours.at[way, number], detour_arrive.at[way, number]).wait()
                    pass_detour(number, group).start()

    def swap(t):
        return pltpu.make_async_remote_copy(
            src_ref=members.at[pl.ds(OWN * REGION + t * GROUP, GROUP)],
            dst_ref=members.at[pl.ds(OTHER * REGION + t * GROUP, GROUP)],
            send_sem=swap_sent.at[t], recv_sem=swap_arrive.at[t],
            device_id=(sibling, z), device_id_type=MESH,
        )

    def start_ships(t):
        for b in (3, 1, 2):
            ship(t, b).start()

    def end_ships(t):
        for b in (3, 1, 2):
            ship(t, b).wait_send()

    def keep(t):
        pass_both(t, 0, block(t, 0))
        pltpu.make_async_copy(block(t, 0), piece(t, OWN, 0), arrive.at[t, 0]).start()

    def relay(t):
        for source in (1, 2, 3):
            arrival(piece(t, OWN, source), arrive.at[t, source]).wait()
            if (t, source) not in DETOURS:
                pass_both(t, source, piece(t, OWN, source))
        start_detours(t)
        arrival(piece(t, OWN, 0), arrive.at[t, 0]).wait()
        swap(t).start()

    def await_near(t):
        for source in range(SIDE):
            for group in (X_PART, Y_PART):
                arrival(piece(t, group, source), near_arrive.at[t, source, group - Y_PART]).wait()

    def tell(step):
        for way in (1, -1):
            pl.semaphore_signal(hello.at[step], inc=1, device_id=(docs, plane(z + way)), device_id_type=MESH)

    def mark(start, size):
        chosen = jnp.where((iota((16, 128), 0) < 8) & (iota((16, 128), 1) == 0), 1.0, 0.0).astype(BF16)
        heads = lax.dot_general(chosen, members[start : start + size, 0:128], NT, preferred_element_type=F32)
        col_bias[:, start : start + size] = jnp.where(heads[0:8] > 1.5, FAR, 0.0)

    def bias_of_rows(start, size):
        first = members[start : start + size, 0:128].astype(F32)[:, 0:1]
        return jnp.where(first > 1.5, FAR, 0.0)

    def scores(base, size, start, width):
        return lax.dot_general(
            members[base : base + size, :], members[start : start + width, :], NT, preferred_element_type=F32
        )

    def along_rows(best, score, start, width):
        biased = score + col_bias[0:1, start : start + width]
        for c in range(0, width, 128):
            best = jnp.maximum(best, biased[:, c : c + 128])
        return best

    def turned(best):
        return jnp.max(best.T, axis=0, keepdims=True)

    def pair_own():
        row_max[...] = jnp.full((REGION, 128), LOWEST, F32)
        for n in range(2 * REGION // 256):
            start = n * 256
            mark(start, 256)
            score = scores(0, REGION, start, 256)
            if start < REGION:
                score = jnp.where(iota((REGION, 256), 0) == iota((REGION, 256), 1) + start, LOWEST, score)
            row_max[...] = along_rows(row_max[...], score, start, 256)
        for t in range(STAGES):
            answer[OWN, t : t + 1] = turned(row_max[t * GROUP : (t + 1) * GROUP, :])

    def pair(base, spans):
        bias = bias_of_rows(base, GROUP)
        best = jnp.full((GROUP, 128), LOWEST, F32)
        for start, width in spans:
            span = pl.ds(start, width)
            score = lax.dot_general(
                members[base : base + GROUP, :], members[span, :], NT, preferred_element_type=F32
            )
            biased = score + col_bias[0:1, span]
            for c in range(0, width, 128):
                best = jnp.maximum(best, biased[:, c : c + 128])
            biased = (score + bias).reshape(GROUP // 8, 8, width)
            col_max[:, span] = jnp.maximum(col_max[:, span], jnp.max(biased, axis=0))
        return turned(best)

    facing = pl.multiple_of(odd_x * REGION, REGION)

    def pair_near(t):
        to_pair_x, to_pair_y = X_PART * REGION + t * GROUP, Y_PART * REGION + t * GROUP
        mark(to_pair_y, GROUP)
        answer[X_PART, t : t + 1] = pair(to_pair_x, [(facing, REGION), (Y_PART * REGION, (t + 1) * GROUP)])
        spans = [(OWN * REGION, REGION)]
        if t:
            spans.append((X_PART * REGION, t * GROUP))
        answer[Y_PART, t : t + 1] = pair(to_pair_y, spans)
        if t + 1 < STAGES:
            mark(to_pair_x, GROUP)

    def hear(step):
        pl.semaphore_wait(hello.at[step], 2)

    start_ships(0)
    keep(0)
    tell(0)
    for t in range(1, STAGES):
        mark_slots(t)
        gather_all()
        scale_slots(t)
        if t in (1, 3):
            start_ships((t + 1) // 2)
        keep(t)
    col_max[...] = jnp.full(col_max.shape, LOWEST, F32)
    answer[...] = jnp.full(answer.shape, LOWEST, F32)
    for t in range(STAGES):
        relay(t)
        if t == 1:
            start_ships(3)
        pass_detours(t)
        if t:
            hear(t - 1)
            tell(t)

    everyone, place_in, _ = ranks(list(range(CLUSTERS)))
    own_rank = jnp.zeros((LINES, 128), F32)
    for number, mask in enumerate(everyone):
        own_rank = own_rank + mask * place_in[number * LINES : (number + 1) * LINES]
    rank_of[...] = own_rank

    for t in range(STAGES):
        swap(t).wait_recv()
    pair_own()
    for t in range(STAGES):
        await_near(t)
        pair_near(t)

    for group in (X_PART, Y_PART, OTHER, OWN):
        for t in range(STAGES):
            start = group * REGION + t * GROUP
            best = jnp.max(col_max[:, start : start + GROUP], axis=0, keepdims=True)
            answer[group, t : t + 1] = jnp.maximum(answer[group, t : t + 1], best)

    def give(group):
        device = {OTHER: sibling, X_PART: to_x, Y_PART: from_y}[group]
        return pltpu.make_async_remote_copy(
            src_ref=answer.at[group], dst_ref=near.at[group], send_sem=near_sent.at[group],
            recv_sem=back_near.at[group], device_id=(device, z), device_id_type=MESH,
        )

    for group in (X_PART, Y_PART, OTHER):
        give(group).start()
    best = answer[OWN]
    for group in (OTHER, X_PART, Y_PART):
        arrival(near.at[group], back_near.at[group]).wait()
        best = jnp.maximum(best, near[group])
    block_of = lax.div(iota((8, 128), 1), PIECE)
    moved = {by: pltpu.roll(best, by * PIECE % 128, 1) for by in range(1 - SIDE, STAGES)}
    for source in range(SIDE):
        spaced = jnp.zeros((8, 128), F32)
        for t in range(STAGES):
            spaced = jnp.where((iota((8, 128), 0) == t) & (block_of == t), moved[t - source], spaced)
        final[source] = jnp.sum(spaced, axis=0, keepdims=True)

    hear(STAGES - 1)

    def spread(source, up):
        return pltpu.make_async_remote_copy(
            src_ref=final.at[source], dst_ref=returned.at[numbers[0]], send_sem=back_sent.at[up, source],
            recv_sem=back_arrive, device_id=(place(*chips[source], core), plane(z + up)), device_id_type=MESH,
        )

    spreads = [spread(source, up) for up in (4, 3, 5, 2, 6, 1, 7, 0) for source in (3, 1, 2, 0) if source or up]
    for copy in spreads:
        copy.start()
    pltpu.make_async_copy(final.at[0], returned.at[numbers[0]], back_arrive).start()

    for group in (OTHER, X_PART, Y_PART):
        give(group).wait_send()

    for t in range(STAGES):
        end_ships(t)
        swap(t).wait_send()
        for group in (X_PART, Y_PART):
            for source in range(SIDE):
                if (t, source) not in DETOURS:
                    pass_on(t, source, piece(t, OWN, source), group).wait_send()
    for number in range(len(DETOURS)):
        for group in (X_PART, Y_PART):
            detour(number, group).wait_send()
            pass_detour(number, group).wait_send()
    for copy in spreads:
        copy.wait_send()
    pltpu.make_async_copy(returned, returned, back_arrive).wait()

    found = returned[...].reshape(CLUSTERS, 128)
    high = found.astype(BF16)
    rest = found - high.astype(F32)
    middle = rest.astype(BF16)
    low = (rest - middle.astype(F32)).astype(BF16)
    parts = jnp.concatenate([high, middle, low], axis=0)
    slot = iota((128, 128), 0).astype(F32)
    line = iota((CLUSTERS, 128), 0)
    for r in range(LINES):
        chosen = jnp.where(slot == rank_of[r : r + 1, :], 1.0, 0.0).astype(BF16)
        taken = jnp.dot(parts, chosen, preferred_element_type=F32)
        taken = taken[0:CLUSTERS] + taken[CLUSTERS : 2 * CLUSTERS] + taken[2 * CLUSTERS :]
        out_ref[r : r + 1] = jnp.sum(
            jnp.where(line == cluster_ref[r : r + 1, :], taken, 0.0), axis=0, keepdims=True
        )


def local(embeds, cluster_of):
    dma = pltpu.SemaphoreType.DMA
    out = pl.pallas_call(
        kernel,
        out_shape=jax.ShapeDtypeStruct((LINES, 128), F32),
        in_specs=[pl.BlockSpec(memory_space=pl.ANY)] * 2,
        out_specs=pl.BlockSpec(memory_space=pltpu.VMEM),
        scratch_shapes=[
            pltpu.VMEM((LINES, 128), jnp.int32),
            pltpu.VMEM((DOCS, WIDTH), BF16),
            pltpu.VMEM((GROUP, DOCS), BF16),
            pltpu.VMEM((GROUP, WIDTH), F32),
            pltpu.VMEM((4 * SLOTS, WIDTH), BF16),
            pltpu.VMEM((MEMBERS, WIDTH), BF16),
            pltpu.VMEM((8, MEMBERS), F32),
            pltpu.VMEM((REGION, 128), F32),
            pltpu.VMEM((8, MEMBERS), F32),
            pltpu.VMEM((4, 8, 128), F32),
            pltpu.VMEM((4, 8, 128), F32),
            pltpu.VMEM((SIDE, 1, 128), F32),
            pltpu.VMEM((CLUSTERS, 1, 128), F32),
            pltpu.VMEM((LINES, 128), F32),
            pltpu.VMEM((2, len(DETOURS), PIECE, WIDTH), BF16),
            dma,
            dma((LOADS,)),
            dma((STAGES, SIDE)),
            dma((STAGES, SIDE)),
            dma((STAGES, SIDE, 2)),
            dma((STAGES, SIDE, 2)),
            dma((STAGES,)),
            dma((STAGES,)),
            dma((4,)),
            dma((4,)),
            dma((PLANES, SIDE)),
            dma,
            pltpu.SemaphoreType.REGULAR((STAGES,)),
            dma((2, len(DETOURS))),
            dma((2, len(DETOURS))),
            dma((2, len(DETOURS))),
        ],
        compiler_params=pltpu.CompilerParams(
            collective_id=0, has_side_effects=True, vmem_limit_bytes=53 * 2**20
        ),
        cost_estimate=pl.CostEstimate(flops=8 * 10**9, bytes_accessed=4 * 2**20, transcendentals=512),
    )(cluster_of.reshape(LINES, 128), embeds)
    return out.reshape(DOCS)


def solution(mesh):
    return jax.shard_map(
        local,
        mesh=mesh,
        in_specs=(P("docs", None), P("docs")),
        out_specs=P("docs"),
        check_vma=False,
    )
```

```python
import jax
import jax.numpy as jnp
from jax import lax
from jax.experimental import pallas as pl
from jax.experimental.pallas import tpu as pltpu
from jax.sharding import PartitionSpec as P


EPSILON = 1e-06
LOWEST = -3e38
FAR = -1e30
PADDED = 2.0

SIDE = 4
PLANES = 8
CLUSTERS = SIDE * PLANES
DOCS = 2048
WIDTH = 1024
SLOTS = 128
STAGES = 4
PIECE = SLOTS // STAGES
GROUP = SIDE * PIECE
REGION = STAGES * GROUP
MEMBERS = 4 * REGION
LOADS = 8
DETOURS = ((0, 3), (1, 3))
LINES = DOCS // 128
OWN, OTHER, Y_PART, X_PART = range(4)

MESH = pl.DeviceIdType.MESH
F32 = jnp.float32
BF16 = jnp.bfloat16
NT = (((1,), (1,)), ((), ()))


def iota(shape, axis):
    return lax.broadcasted_iota(jnp.int32, shape, axis)


def kernel(
    cluster_hbm, embeds_ref, out_ref,
    cluster_ref, rows, pick, gathered, blocks, members, col_bias, row_max, col_max, answer,
    near, final, returned, rank_of, detours,
    cluster_sem, load_sem, shipped, arrive, passed, near_arrive, swap_sent, swap_arrive, near_sent, back_near, back_sent,
    back_arrive, hello, detour_sent, detour_arrive, detour_passed,
):
    docs = lax.axis_index("docs")
    z = lax.axis_index("grp")
    core = lax.rem(docs, 2)
    x = lax.rem(lax.div(docs, 2), SIDE)
    y = lax.div(docs, 2 * SIDE)

    def place(px, py, pcore):
        return (lax.rem(py + SIDE, SIDE) * SIDE + lax.rem(px + SIDE, SIDE)) * 2 + lax.rem(pcore, 2)

    def plane(pz):
        return lax.rem(pz + PLANES, PLANES)

    shifted = lax.rem(z, 2)
    odd_x = lax.rem(x + shifted, 2)
    odd_y = lax.rem(y + shifted, 2)
    in_x, out_x = x + 1 - 2 * odd_x, x - 1 + 2 * odd_x
    in_y, out_y = y + 1 - 2 * odd_y, y - 1 + 2 * odd_y

    def cluster_at(px, py):
        tile_x = lax.div(lax.rem(px + SIDE - shifted, SIDE), 2)
        tile_y = lax.div(lax.rem(py + SIDE - shifted, SIDE), 2)
        return SIDE * z + 2 * tile_y + tile_x

    chips = [(x, y), (out_x, y), (x, out_y), (out_x, out_y)]
    numbers = [cluster_at(px + SIDE, py + SIDE) for px, py in chips]

    sibling = place(x, y, core + 1)
    to_x = place(in_x, y, core)
    to_y = place(x, in_y, core + 1 - odd_y)
    from_y = place(x, in_y, core + odd_y)

    cluster_load = pltpu.make_async_copy(cluster_hbm, cluster_ref, cluster_sem)
    cluster_load.start()
    loads = []
    for part in range(LOADS):
        span = pl.ds(part * (DOCS // LOADS), DOCS // LOADS)
        loads.append(pltpu.make_async_copy(embeds_ref.at[span], rows.at[span], load_sem.at[part]))
        loads[-1].start()

    barrier = pltpu.get_barrier_semaphore()

    def greet(device):
        pl.semaphore_signal(barrier, inc=1, device_id=device, device_id_type=MESH)

    greet((place(out_x, y, core), plane(z - 1)))
    greet((place(x, out_y, core + 1 - odd_y), plane(z + 1)))
    for dx in (-1, 0, 1):
        for dy in (-1, 0, 1):
            if dx or dy:
                greet((place(x + dx, y + dy, core), z))
    greet((place(x, y + 1, core + 1), z))
    greet((place(x, y - 1, core + 1), z))
    greet((sibling, z))
    greet((docs, plane(z + 1)))
    greet((docs, plane(z - 1)))

    cluster_load.wait()
    clusters = cluster_ref[...]

    def ranks(numbers):
        member = [jnp.where(clusters == number, 1.0, 0.0).astype(F32) for number in numbers]
        stacked = jnp.concatenate(member, axis=0).astype(BF16)
        before = jnp.where(iota((128, 128), 0) < iota((128, 128), 1), 1.0, 0.0).astype(BF16)
        within = jnp.dot(stacked, before, preferred_element_type=F32)
        totals = jnp.dot(stacked, jnp.ones((128, 128), BF16), preferred_element_type=F32)
        lines = len(member) * LINES
        above = (iota((lines, lines), 1) < iota((lines, lines), 0)) & (
            lax.div(iota((lines, lines), 1), LINES) == lax.div(iota((lines, lines), 0), LINES)
        )
        offsets = jnp.dot(
            jnp.where(above, 1.0, 0.0).astype(BF16), totals.astype(BF16), preferred_element_type=F32
        )
        return member, within + offsets, totals

    member, rank, totals = ranks(numbers)
    positions = [jnp.where(member[b] > 0, rank[b * LINES : (b + 1) * LINES], -1.0) for b in range(4)]
    counts = [jnp.sum(totals[b * LINES : (b + 1) * LINES], axis=0, keepdims=True) for b in range(4)]

    def mark_slots(t):
        slot = iota((PIECE, 128), 0).astype(F32) + t * PIECE
        for b in range(4):
            for r in range(LINES):
                pick[b * PIECE : (b + 1) * PIECE, r * 128 : (r + 1) * 128] = jnp.where(
                    slot == positions[b][r : r + 1], 1.0, 0.0
                ).astype(BF16)

    def scale_slots(t):
        slot = iota((PIECE, 128), 0).astype(F32) + t * PIECE
        for b in range(4):
            values = gathered[b * PIECE : (b + 1) * PIECE, :]
            inverse = lax.rsqrt(jnp.sum(values * values, axis=1, keepdims=True) + EPSILON)
            scaled = values * inverse
            empty = (slot >= counts[b]) & (iota((PIECE, 128), 1) == 0)
            at = (t * 4 + b) * PIECE
            blocks[at : at + PIECE, :] = scaled.astype(BF16)
            blocks[at : at + PIECE, 0:128] = jnp.where(empty, PADDED, scaled[:, 0:128]).astype(BF16)

    def gather_part(part):
        span = slice(part * (DOCS // LOADS), (part + 1) * (DOCS // LOADS))
        for c in range(0, WIDTH, 256):
            taken = jnp.dot(pick[:, span], rows[span, c : c + 256], preferred_element_type=F32)
            gathered[:, c : c + 256] = taken if part == 0 else gathered[:, c : c + 256] + taken

    def gather_all():
        def gather(n, carry):
            cols = pl.ds(pl.multiple_of(n * 256, 256), 256)
            gathered[:, cols] = jnp.dot(pick[...], rows[:, cols], preferred_element_type=F32)
            return carry

        lax.fori_loop(0, WIDTH // 256, gather, 0)

    mark_slots(0)
    for part in range(LOADS):
        loads[part].wait()
        gather_part(part)
    scale_slots(0)
    pl.semaphore_wait(barrier, 15)

    def piece(t, group, source):
        return members.at[pl.ds(pl.multiple_of(group * REGION + t * GROUP + source * PIECE, PIECE), PIECE)]

    def block(t, b):
        return blocks.at[pl.ds(pl.multiple_of((t * 4 + b) * PIECE, PIECE), PIECE)]

    def arrival(ref, sem):
        return pltpu.make_async_copy(ref, ref, sem)

    def ship(t, b):
        return pltpu.make_async_remote_copy(
            src_ref=block(t, b), dst_ref=piece(t, OWN, b), send_sem=shipped.at[t, b], recv_sem=arrive.at[t, b],
            device_id=(place(*chips[b], core), z), device_id_type=MESH,
        )

    def pass_on(t, source, src, group):
        return pltpu.make_async_remote_copy(
            src_ref=src, dst_ref=piece(t, group, source),
            send_sem=passed.at[t, source, group - Y_PART], recv_sem=near_arrive.at[t, source, group - Y_PART],
            device_id=(to_x if group == X_PART else to_y, z), device_id_type=MESH,
        )

    def pass_both(t, source, src):
        pass_on(t, source, src, X_PART).start()
        pass_on(t, source, src, Y_PART).start()

    def detour(number, group):
        (t, source), way = DETOURS[number], group - Y_PART
        return pltpu.make_async_remote_copy(
            src_ref=piece(t, OWN, source), dst_ref=detours.at[way, number],
            send_sem=detour_sent.at[way, number], recv_sem=detour_arrive.at[way, number],
            device_id=(to_x, plane(z + 1)) if group == X_PART else (to_y, plane(z - 1)), device_id_type=MESH,
        )

    def pass_detour(number, group):
        (t, source), way = DETOURS[number], group - Y_PART
        return pltpu.make_async_remote_copy(
            src_ref=detours.at[way, number], dst_ref=piece(t, group, source),
            send_sem=detour_passed.at[way, number], recv_sem=near_arrive.at[t, source, way],
            device_id=(docs, plane(z - 1) if group == X_PART else plane(z + 1)), device_id_type=MESH,
        )

    def start_detours(t):
        for number, (stage, source) in enumerate(DETOURS):
            if stage == t:
                detour(number, X_PART).start()
                detour(number, Y_PART).start()

    def pass_detours(t):
        for number, (stage, source) in enumerate(DETOURS):
            if t == min(stage + 2, STAGES - 1):
                for group in (X_PART, Y_PART):
                    way = group - Y_PART
                    arrival(detours.at[way, number], detour_arrive.at[way, number]).wait()
                    pass_detour(number, group).start()

    def swap(t):
        return pltpu.make_async_remote_copy(
            src_ref=members.at[pl.ds(OWN * REGION + t * GROUP, GROUP)],
            dst_ref=members.at[pl.ds(OTHER * REGION + t * GROUP, GROUP)],
            send_sem=swap_sent.at[t], recv_sem=swap_arrive.at[t],
            device_id=(sibling, z), device_id_type=MESH,
        )

    def start_ships(t):
        for b in (3, 1, 2):
            ship(t, b).start()

    def end_ships(t):
        for b in (3, 1, 2):
            ship(t, b).wait_send()

    def keep(t):
        pass_both(t, 0, block(t, 0))
        pltpu.make_async_copy(block(t, 0), piece(t, OWN, 0), arrive.at[t, 0]).start()

    def relay(t):
        for source in (1, 2, 3):
            arrival(piece(t, OWN, source), arrive.at[t, source]).wait()
            if (t, source) not in DETOURS:
                pass_both(t, source, piece(t, OWN, source))
        start_detours(t)
        arrival(piece(t, OWN, 0), arrive.at[t, 0]).wait()
        swap(t).start()

    def await_near(t):
        for source in range(SIDE):
            for group in (X_PART, Y_PART):
                arrival(piece(t, group, source), near_arrive.at[t, source, group - Y_PART]).wait()

    def tell(step):
        for way in (1, -1):
            pl.semaphore_signal(hello.at[step], inc=1, device_id=(docs, plane(z + way)), device_id_type=MESH)

    def mark(start, size):
        chosen = jnp.where((iota((16, 128), 0) < 8) & (iota((16, 128), 1) == 0), 1.0, 0.0).astype(BF16)
        heads = lax.dot_general(chosen, members[start : start + size, 0:128], NT, preferred_element_type=F32)
        col_bias[:, start : start + size] = jnp.where(heads[0:8] > 1.5, FAR, 0.0)

    def bias_of_rows(start, size):
        first = members[start : start + size, 0:128].astype(F32)[:, 0:1]
        return jnp.where(first > 1.5, FAR, 0.0)

    def scores(base, size, start, width):
        return lax.dot_general(
            members[base : base + size, :], members[start : start + width, :], NT, preferred_element_type=F32
        )

    def along_rows(best, score, start, width):
        biased = score + col_bias[0:1, start : start + width]
        for c in range(0, width, 128):
            best = jnp.maximum(best, biased[:, c : c + 128])
        return best

    def turned(best):
        return jnp.max(best.T, axis=0, keepdims=True)

    def pair_own():
        row_max[...] = jnp.full((REGION, 128), LOWEST, F32)
        for n in range(2 * REGION // 256):
            start = n * 256
            mark(start, 256)
            score = scores(0, REGION, start, 256)
            if start < REGION:
                score = jnp.where(iota((REGION, 256), 0) == iota((REGION, 256), 1) + start, LOWEST, score)
            row_max[...] = along_rows(row_max[...], score, start, 256)
        for t in range(STAGES):
            answer[OWN, t : t + 1] = turned(row_max[t * GROUP : (t + 1) * GROUP, :])

    def pair(base, spans):
        bias = bias_of_rows(base, GROUP)
        best = jnp.full((GROUP, 128), LOWEST, F32)
        for start, width in spans:
            span = pl.ds(start, width)
            score = lax.dot_general(
                members[base : base + GROUP, :], members[span, :], NT, preferred_element_type=F32
            )
            biased = score + col_bias[0:1, span]
            for c in range(0, width, 128):
                best = jnp.maximum(best, biased[:, c : c + 128])
            biased = (score + bias).reshape(GROUP // 8, 8, width)
            col_max[:, span] = jnp.maximum(col_max[:, span], jnp.max(biased, axis=0))
        return turned(best)

    facing = pl.multiple_of(odd_x * REGION, REGION)

    def pair_near(t):
        to_pair_x, to_pair_y = X_PART * REGION + t * GROUP, Y_PART * REGION + t * GROUP
        mark(to_pair_y, GROUP)
        answer[X_PART, t : t + 1] = pair(to_pair_x, [(facing, REGION), (Y_PART * REGION, (t + 1) * GROUP)])
        spans = [(OWN * REGION, REGION)]
        if t:
            spans.append((X_PART * REGION, t * GROUP))
        answer[Y_PART, t : t + 1] = pair(to_pair_y, spans)
        if t + 1 < STAGES:
            mark(to_pair_x, GROUP)

    def hear(step):
        pl.semaphore_wait(hello.at[step], 2)

    start_ships(0)
    keep(0)
    tell(0)
    for t in range(1, STAGES):
        mark_slots(t)
        gather_all()
        scale_slots(t)
        if t in (1, 3):
            start_ships((t + 1) // 2)
        keep(t)
    col_max[...] = jnp.full(col_max.shape, LOWEST, F32)
    answer[...] = jnp.full(answer.shape, LOWEST, F32)
    everyone, place_in, _ = ranks(list(range(CLUSTERS)))
    own_rank = jnp.zeros((LINES, 128), F32)
    for number, mask in enumerate(everyone):
        own_rank = own_rank + mask * place_in[number * LINES : (number + 1) * LINES]
    rank_of[...] = own_rank

    for t in range(STAGES):
        relay(t)
        if t == 1:
            start_ships(3)
        pass_detours(t)
        if t:
            hear(t - 1)
            tell(t)

    for t in range(STAGES):
        swap(t).wait_recv()
    pair_own()
    for t in range(STAGES):
        await_near(t)
        pair_near(t)

    for group in (X_PART, Y_PART, OTHER, OWN):
        for t in range(STAGES):
            start = group * REGION + t * GROUP
            best = jnp.max(col_max[:, start : start + GROUP], axis=0, keepdims=True)
            answer[group, t : t + 1] = jnp.maximum(answer[group, t : t + 1], best)

    def give(group):
        device = {OTHER: sibling, X_PART: to_x, Y_PART: from_y}[group]
        return pltpu.make_async_remote_copy(
            src_ref=answer.at[group], dst_ref=near.at[group], send_sem=near_sent.at[group],
            recv_sem=back_near.at[group], device_id=(device, z), device_id_type=MESH,
        )

    for group in (X_PART, Y_PART, OTHER):
        give(group).start()
    best = answer[OWN]
    for group in (OTHER, X_PART, Y_PART):
        arrival(near.at[group], back_near.at[group]).wait()
        best = jnp.maximum(best, near[group])
    block_of = lax.div(iota((8, 128), 1), PIECE)
    moved = {by: pltpu.roll(best, by * PIECE % 128, 1) for by in range(1 - SIDE, STAGES)}
    for source in range(SIDE):
        spaced = jnp.zeros((8, 128), F32)
        for t in range(STAGES):
            spaced = jnp.where((iota((8, 128), 0) == t) & (block_of == t), moved[t - source], spaced)
        final[source] = jnp.sum(spaced, axis=0, keepdims=True)

    hear(STAGES - 1)

    def spread(source, up):
        return pltpu.make_async_remote_copy(
            src_ref=final.at[source], dst_ref=returned.at[numbers[0]], send_sem=back_sent.at[up, source],
            recv_sem=back_arrive, device_id=(place(*chips[source], core), plane(z + up)), device_id_type=MESH,
        )

    spreads = [spread(source, up) for up in (4, 3, 5, 2, 6, 1, 7, 0) for source in (3, 1, 2, 0) if source or up]
    for copy in spreads:
        copy.start()
    pltpu.make_async_copy(final.at[0], returned.at[numbers[0]], back_arrive).start()

    for group in (OTHER, X_PART, Y_PART):
        give(group).wait_send()

    for t in range(STAGES):
        end_ships(t)
        swap(t).wait_send()
        for group in (X_PART, Y_PART):
            for source in range(SIDE):
                if (t, source) not in DETOURS:
                    pass_on(t, source, piece(t, OWN, source), group).wait_send()
    for number in range(len(DETOURS)):
        for group in (X_PART, Y_PART):
            detour(number, group).wait_send()
            pass_detour(number, group).wait_send()
    for copy in spreads:
        copy.wait_send()
    pltpu.make_async_copy(returned, returned, back_arrive).wait()

    found = returned[...].reshape(CLUSTERS, 128)
    high = found.astype(BF16)
    rest = found - high.astype(F32)
    middle = rest.astype(BF16)
    low = (rest - middle.astype(F32)).astype(BF16)
    parts = jnp.concatenate([high, middle, low], axis=0)
    slot = iota((128, 128), 0).astype(F32)
    line = iota((CLUSTERS, 128), 0)
    for r in range(LINES):
        chosen = jnp.where(slot == rank_of[r : r + 1, :], 1.0, 0.0).astype(BF16)
        taken = jnp.dot(parts, chosen, preferred_element_type=F32)
        taken = taken[0:CLUSTERS] + taken[CLUSTERS : 2 * CLUSTERS] + taken[2 * CLUSTERS :]
        out_ref[r : r + 1] = jnp.sum(
            jnp.where(line == cluster_ref[r : r + 1, :], taken, 0.0), axis=0, keepdims=True
        )


def local(embeds, cluster_of):
    dma = pltpu.SemaphoreType.DMA
    out = pl.pallas_call(
        kernel,
        out_shape=jax.ShapeDtypeStruct((LINES, 128), F32),
        in_specs=[pl.BlockSpec(memory_space=pl.ANY)] * 2,
        out_specs=pl.BlockSpec(memory_space=pltpu.VMEM),
        scratch_shapes=[
            pltpu.VMEM((LINES, 128), jnp.int32),
            pltpu.VMEM((DOCS, WIDTH), BF16),
            pltpu.VMEM((GROUP, DOCS), BF16),
            pltpu.VMEM((GROUP, WIDTH), F32),
            pltpu.VMEM((4 * SLOTS, WIDTH), BF16),
            pltpu.VMEM((MEMBERS, WIDTH), BF16),
            pltpu.VMEM((8, MEMBERS), F32),
            pltpu.VMEM((REGION, 128), F32),
            pltpu.VMEM((8, MEMBERS), F32),
            pltpu.VMEM((4, 8, 128), F32),
            pltpu.VMEM((4, 8, 128), F32),
            pltpu.VMEM((SIDE, 1, 128), F32),
            pltpu.VMEM((CLUSTERS, 1, 128), F32),
            pltpu.VMEM((LINES, 128), F32),
            pltpu.VMEM((2, len(DETOURS), PIECE, WIDTH), BF16),
            dma,
            dma((LOADS,)),
            dma((STAGES, SIDE)),
            dma((STAGES, SIDE)),
            dma((STAGES, SIDE, 2)),
            dma((STAGES, SIDE, 2)),
            dma((STAGES,)),
            dma((STAGES,)),
            dma((4,)),
            dma((4,)),
            dma((PLANES, SIDE)),
            dma,
            pltpu.SemaphoreType.REGULAR((STAGES,)),
            dma((2, len(DETOURS))),
            dma((2, len(DETOURS))),
            dma((2, len(DETOURS))),
        ],
        compiler_params=pltpu.CompilerParams(
            collective_id=0, has_side_effects=True, vmem_limit_bytes=53 * 2**20
        ),
        cost_estimate=pl.CostEstimate(flops=8 * 10**9, bytes_accessed=4 * 2**20, transcendentals=512),
    )(cluster_of.reshape(LINES, 128), embeds)
    return out.reshape(DOCS)


def solution(mesh):
    return jax.shard_map(
        local,
        mesh=mesh,
        in_specs=(P("docs", None), P("docs")),
        out_specs=P("docs"),
        check_vma=False,
    )
```

```python
import jax
import jax.numpy as jnp
from jax import lax
from jax.experimental import pallas as pl
from jax.experimental.pallas import tpu as pltpu
from jax.sharding import PartitionSpec as P


EPSILON = 1e-06
LOWEST = -3e38
FAR = -1e30
PADDED = 2.0

SIDE = 4
PLANES = 8
CLUSTERS = SIDE * PLANES
DOCS = 2048
WIDTH = 1024
SLOTS = 128
STAGES = 4
PIECE = SLOTS // STAGES
GROUP = SIDE * PIECE
REGION = STAGES * GROUP
MEMBERS = 4 * REGION
LOADS = 4
DETOURS = ((0, 3), (1, 3))
LINES = DOCS // 128
OWN, OTHER, Y_PART, X_PART = range(4)

MESH = pl.DeviceIdType.MESH
F32 = jnp.float32
BF16 = jnp.bfloat16
NT = (((1,), (1,)), ((), ()))


def iota(shape, axis):
    return lax.broadcasted_iota(jnp.int32, shape, axis)


def kernel(
    cluster_hbm, embeds_ref, out_ref,
    cluster_ref, rows, pick, gathered, blocks, members, col_bias, row_max, col_max, answer,
    near, final, returned, rank_of, detours,
    cluster_sem, load_sem, shipped, arrive, passed, near_arrive, swap_sent, swap_arrive, near_sent, back_near, back_sent,
    back_arrive, hello, detour_sent, detour_arrive, detour_passed,
):
    docs = lax.axis_index("docs")
    z = lax.axis_index("grp")
    core = lax.rem(docs, 2)
    x = lax.rem(lax.div(docs, 2), SIDE)
    y = lax.div(docs, 2 * SIDE)

    def place(px, py, pcore):
        return (lax.rem(py + SIDE, SIDE) * SIDE + lax.rem(px + SIDE, SIDE)) * 2 + lax.rem(pcore, 2)

    def plane(pz):
        return lax.rem(pz + PLANES, PLANES)

    shifted = lax.rem(z, 2)
    odd_x = lax.rem(x + shifted, 2)
    odd_y = lax.rem(y + shifted, 2)
    in_x, out_x = x + 1 - 2 * odd_x, x - 1 + 2 * odd_x
    in_y, out_y = y + 1 - 2 * odd_y, y - 1 + 2 * odd_y

    def cluster_at(px, py):
        tile_x = lax.div(lax.rem(px + SIDE - shifted, SIDE), 2)
        tile_y = lax.div(lax.rem(py + SIDE - shifted, SIDE), 2)
        return SIDE * z + 2 * tile_y + tile_x

    chips = [(x, y), (out_x, y), (x, out_y), (out_x, out_y)]
    numbers = [cluster_at(px + SIDE, py + SIDE) for px, py in chips]

    sibling = place(x, y, core + 1)
    to_x = place(in_x, y, core)
    to_y = place(x, in_y, core + 1 - odd_y)
    from_y = place(x, in_y, core + odd_y)

    cluster_load = pltpu.make_async_copy(cluster_hbm, cluster_ref, cluster_sem)
    cluster_load.start()
    loads = []
    for part in range(LOADS):
        span = pl.ds(part * (DOCS // LOADS), DOCS // LOADS)
        loads.append(pltpu.make_async_copy(embeds_ref.at[span], rows.at[span], load_sem.at[part]))
        loads[-1].start()

    barrier = pltpu.get_barrier_semaphore()

    def greet(device):
        pl.semaphore_signal(barrier, inc=1, device_id=device, device_id_type=MESH)

    greet((place(out_x, y, core), plane(z - 1)))
    greet((place(x, out_y, core + 1 - odd_y), plane(z + 1)))
    for dx in (-1, 0, 1):
        for dy in (-1, 0, 1):
            if dx or dy:
                greet((place(x + dx, y + dy, core), z))
    greet((place(x, y + 1, core + 1), z))
    greet((place(x, y - 1, core + 1), z))
    greet((sibling, z))
    greet((docs, plane(z + 1)))
    greet((docs, plane(z - 1)))

    cluster_load.wait()
    clusters = cluster_ref[...]

    def ranks(numbers):
        member = [jnp.where(clusters == number, 1.0, 0.0).astype(F32) for number in numbers]
        stacked = jnp.concatenate(member, axis=0).astype(BF16)
        before = jnp.where(iota((128, 128), 0) < iota((128, 128), 1), 1.0, 0.0).astype(BF16)
        within = jnp.dot(stacked, before, preferred_element_type=F32)
        totals = jnp.dot(stacked, jnp.ones((128, 128), BF16), preferred_element_type=F32)
        lines = len(member) * LINES
        above = (iota((lines, lines), 1) < iota((lines, lines), 0)) & (
            lax.div(iota((lines, lines), 1), LINES) == lax.div(iota((lines, lines), 0), LINES)
        )
        offsets = jnp.dot(
            jnp.where(above, 1.0, 0.0).astype(BF16), totals.astype(BF16), preferred_element_type=F32
        )
        return member, within + offsets, totals

    member, rank, totals = ranks(numbers)
    positions = [jnp.where(member[b] > 0, rank[b * LINES : (b + 1) * LINES], -1.0) for b in range(4)]
    counts = [jnp.sum(totals[b * LINES : (b + 1) * LINES], axis=0, keepdims=True) for b in range(4)]

    def mark_slots(t):
        slot = iota((PIECE, 128), 0).astype(F32) + t * PIECE
        for b in range(4):
            for r in range(LINES):
                pick[b * PIECE : (b + 1) * PIECE, r * 128 : (r + 1) * 128] = jnp.where(
                    slot == positions[b][r : r + 1], 1.0, 0.0
                ).astype(BF16)

    def scale_slots(t):
        slot = iota((PIECE, 128), 0).astype(F32) + t * PIECE
        for b in range(4):
            values = gathered[b * PIECE : (b + 1) * PIECE, :]
            inverse = lax.rsqrt(jnp.sum(values * values, axis=1, keepdims=True) + EPSILON)
            scaled = values * inverse
            empty = (slot >= counts[b]) & (iota((PIECE, 128), 1) == 0)
            at = (t * 4 + b) * PIECE
            blocks[at : at + PIECE, :] = scaled.astype(BF16)
            blocks[at : at + PIECE, 0:128] = jnp.where(empty, PADDED, scaled[:, 0:128]).astype(BF16)

    def gather_part(part):
        span = slice(part * (DOCS // LOADS), (part + 1) * (DOCS // LOADS))
        for c in range(0, WIDTH, 256):
            taken = jnp.dot(pick[:, span], rows[span, c : c + 256], preferred_element_type=F32)
            gathered[:, c : c + 256] = taken if part == 0 else gathered[:, c : c + 256] + taken

    def gather_all():
        def gather(n, carry):
            cols = pl.ds(pl.multiple_of(n * 256, 256), 256)
            gathered[:, cols] = jnp.dot(pick[...], rows[:, cols], preferred_element_type=F32)
            return carry

        lax.fori_loop(0, WIDTH // 256, gather, 0)

    mark_slots(0)
    for part in range(LOADS):
        loads[part].wait()
        gather_part(part)
    scale_slots(0)
    pl.semaphore_wait(barrier, 15)

    def piece(t, group, source):
        return members.at[pl.ds(pl.multiple_of(group * REGION + t * GROUP + source * PIECE, PIECE), PIECE)]

    def block(t, b):
        return blocks.at[pl.ds(pl.multiple_of((t * 4 + b) * PIECE, PIECE), PIECE)]

    def arrival(ref, sem):
        return pltpu.make_async_copy(ref, ref, sem)

    def ship(t, b):
        return pltpu.make_async_remote_copy(
            src_ref=block(t, b), dst_ref=piece(t, OWN, b), send_sem=shipped.at[t, b], recv_sem=arrive.at[t, b],
            device_id=(place(*chips[b], core), z), device_id_type=MESH,
        )

    def pass_on(t, source, src, group):
        return pltpu.make_async_remote_copy(
            src_ref=src, dst_ref=piece(t, group, source),
            send_sem=passed.at[t, source, group - Y_PART], recv_sem=near_arrive.at[t, source, group - Y_PART],
            device_id=(to_x if group == X_PART else to_y, z), device_id_type=MESH,
        )

    def pass_both(t, source, src):
        pass_on(t, source, src, X_PART).start()
        pass_on(t, source, src, Y_PART).start()

    def detour(number, group):
        (t, source), way = DETOURS[number], group - Y_PART
        return pltpu.make_async_remote_copy(
            src_ref=piece(t, OWN, source), dst_ref=detours.at[way, number],
            send_sem=detour_sent.at[way, number], recv_sem=detour_arrive.at[way, number],
            device_id=(to_x, plane(z + 1)) if group == X_PART else (to_y, plane(z - 1)), device_id_type=MESH,
        )

    def pass_detour(number, group):
        (t, source), way = DETOURS[number], group - Y_PART
        return pltpu.make_async_remote_copy(
            src_ref=detours.at[way, number], dst_ref=piece(t, group, source),
            send_sem=detour_passed.at[way, number], recv_sem=near_arrive.at[t, source, way],
            device_id=(docs, plane(z - 1) if group == X_PART else plane(z + 1)), device_id_type=MESH,
        )

    def start_detours(t):
        for number, (stage, source) in enumerate(DETOURS):
            if stage == t:
                detour(number, X_PART).start()
                detour(number, Y_PART).start()

    def pass_detours(t):
        for number, (stage, source) in enumerate(DETOURS):
            if t == min(stage + 2, STAGES - 1):
                for group in (X_PART, Y_PART):
                    way = group - Y_PART
                    arrival(detours.at[way, number], detour_arrive.at[way, number]).wait()
                    pass_detour(number, group).start()

    def swap(t):
        return pltpu.make_async_remote_copy(
            src_ref=members.at[pl.ds(OWN * REGION + t * GROUP, GROUP)],
            dst_ref=members.at[pl.ds(OTHER * REGION + t * GROUP, GROUP)],
            send_sem=swap_sent.at[t], recv_sem=swap_arrive.at[t],
            device_id=(sibling, z), device_id_type=MESH,
        )

    def start_ships(t):
        for b in (3, 1, 2):
            ship(t, b).start()

    def end_ships(t):
        for b in (3, 1, 2):
            ship(t, b).wait_send()

    def keep(t):
        pass_both(t, 0, block(t, 0))
        pltpu.make_async_copy(block(t, 0), piece(t, OWN, 0), arrive.at[t, 0]).start()

    def relay(t):
        for source in (1, 2, 3):
            arrival(piece(t, OWN, source), arrive.at[t, source]).wait()
            if (t, source) not in DETOURS:
                pass_both(t, source, piece(t, OWN, source))
        start_detours(t)
        arrival(piece(t, OWN, 0), arrive.at[t, 0]).wait()
        swap(t).start()

    def await_near(t):
        for source in range(SIDE):
            for group in (X_PART, Y_PART):
                arrival(piece(t, group, source), near_arrive.at[t, source, group - Y_PART]).wait()

    def tell(step):
        for way in (1, -1):
            pl.semaphore_signal(hello.at[step], inc=1, device_id=(docs, plane(z + way)), device_id_type=MESH)

    def mark(start, size):
        chosen = jnp.where((iota((16, 128), 0) < 8) & (iota((16, 128), 1) == 0), 1.0, 0.0).astype(BF16)
        heads = lax.dot_general(chosen, members[start : start + size, 0:128], NT, preferred_element_type=F32)
        col_bias[:, start : start + size] = jnp.where(heads[0:8] > 1.5, FAR, 0.0)

    def bias_of_rows(start, size):
        first = members[start : start + size, 0:128].astype(F32)[:, 0:1]
        return jnp.where(first > 1.5, FAR, 0.0)

    def scores(base, size, start, width):
        return lax.dot_general(
            members[base : base + size, :], members[start : start + width, :], NT, preferred_element_type=F32
        )

    def along_rows(best, score, start, width):
        biased = score + col_bias[0:1, start : start + width]
        for c in range(0, width, 128):
            best = jnp.maximum(best, biased[:, c : c + 128])
        return best

    def turned(best):
        return jnp.max(best.T, axis=0, keepdims=True)

    def pair_own():
        row_max[...] = jnp.full((REGION, 128), LOWEST, F32)
        for n in range(2 * REGION // 256):
            start = n * 256
            mark(start, 256)
            score = scores(0, REGION, start, 256)
            if start < REGION:
                score = jnp.where(iota((REGION, 256), 0) == iota((REGION, 256), 1) + start, LOWEST, score)
            row_max[...] = along_rows(row_max[...], score, start, 256)
        for t in range(STAGES):
            answer[OWN, t : t + 1] = turned(row_max[t * GROUP : (t + 1) * GROUP, :])

    def pair(base, spans):
        bias = bias_of_rows(base, GROUP)
        best = jnp.full((GROUP, 128), LOWEST, F32)
        for start, width in spans:
            span = pl.ds(start, width)
            score = lax.dot_general(
                members[base : base + GROUP, :], members[span, :], NT, preferred_element_type=F32
            )
            biased = score + col_bias[0:1, span]
            for c in range(0, width, 128):
                best = jnp.maximum(best, biased[:, c : c + 128])
            biased = (score + bias).reshape(GROUP // 8, 8, width)
            col_max[:, span] = jnp.maximum(col_max[:, span], jnp.max(biased, axis=0))
        return turned(best)

    facing = pl.multiple_of(odd_x * REGION, REGION)

    def pair_near(t):
        to_pair_x, to_pair_y = X_PART * REGION + t * GROUP, Y_PART * REGION + t * GROUP
        mark(to_pair_y, GROUP)
        answer[X_PART, t : t + 1] = pair(to_pair_x, [(facing, REGION), (Y_PART * REGION, (t + 1) * GROUP)])
        spans = [(OWN * REGION, REGION)]
        if t:
            spans.append((X_PART * REGION, t * GROUP))
        answer[Y_PART, t : t + 1] = pair(to_pair_y, spans)
        if t + 1 < STAGES:
            mark(to_pair_x, GROUP)

    def hear(step):
        pl.semaphore_wait(hello.at[step], 2)

    start_ships(0)
    keep(0)
    tell(0)
    for t in range(1, STAGES):
        mark_slots(t)
        gather_all()
        scale_slots(t)
        if t in (1, 3):
            start_ships((t + 1) // 2)
        keep(t)
    col_max[...] = jnp.full(col_max.shape, LOWEST, F32)
    answer[...] = jnp.full(answer.shape, LOWEST, F32)
    everyone, place_in, _ = ranks(list(range(CLUSTERS)))
    own_rank = jnp.zeros((LINES, 128), F32)
    for number, mask in enumerate(everyone):
        own_rank = own_rank + mask * place_in[number * LINES : (number + 1) * LINES]
    rank_of[...] = own_rank

    for t in range(STAGES):
        relay(t)
        if t == 1:
            start_ships(3)
        pass_detours(t)
        if t:
            hear(t - 1)
            tell(t)

    for t in range(STAGES):
        swap(t).wait_recv()
    pair_own()
    for t in range(STAGES):
        await_near(t)
        pair_near(t)

    for group in (X_PART, Y_PART, OTHER, OWN):
        for t in range(STAGES):
            start = group * REGION + t * GROUP
            best = jnp.max(col_max[:, start : start + GROUP], axis=0, keepdims=True)
            answer[group, t : t + 1] = jnp.maximum(answer[group, t : t + 1], best)

    def give(group):
        device = {OTHER: sibling, X_PART: to_x, Y_PART: from_y}[group]
        return pltpu.make_async_remote_copy(
            src_ref=answer.at[group], dst_ref=near.at[group], send_sem=near_sent.at[group],
            recv_sem=back_near.at[group], device_id=(device, z), device_id_type=MESH,
        )

    for group in (X_PART, Y_PART, OTHER):
        give(group).start()
    best = answer[OWN]
    for group in (OTHER, X_PART, Y_PART):
        arrival(near.at[group], back_near.at[group]).wait()
        best = jnp.maximum(best, near[group])
    block_of = lax.div(iota((8, 128), 1), PIECE)
    moved = {by: pltpu.roll(best, by * PIECE % 128, 1) for by in range(1 - SIDE, STAGES)}
    for source in range(SIDE):
        spaced = jnp.zeros((8, 128), F32)
        for t in range(STAGES):
            spaced = jnp.where((iota((8, 128), 0) == t) & (block_of == t), moved[t - source], spaced)
        final[source] = jnp.sum(spaced, axis=0, keepdims=True)

    hear(STAGES - 1)

    def spread(source, up):
        return pltpu.make_async_remote_copy(
            src_ref=final.at[source], dst_ref=returned.at[numbers[0]], send_sem=back_sent.at[up, source],
            recv_sem=back_arrive, device_id=(place(*chips[source], core), plane(z + up)), device_id_type=MESH,
        )

    spreads = [spread(source, up) for up in (4, 3, 5, 2, 6, 1, 7, 0) for source in (3, 1, 2, 0) if source or up]
    for copy in spreads:
        copy.start()
    pltpu.make_async_copy(final.at[0], returned.at[numbers[0]], back_arrive).start()

    for group in (OTHER, X_PART, Y_PART):
        give(group).wait_send()

    for t in range(STAGES):
        end_ships(t)
        swap(t).wait_send()
        for group in (X_PART, Y_PART):
            for source in range(SIDE):
                if (t, source) not in DETOURS:
                    pass_on(t, source, piece(t, OWN, source), group).wait_send()
    for number in range(len(DETOURS)):
        for group in (X_PART, Y_PART):
            detour(number, group).wait_send()
            pass_detour(number, group).wait_send()
    for copy in spreads:
        copy.wait_send()
    pltpu.make_async_copy(returned, returned, back_arrive).wait()

    found = returned[...].reshape(CLUSTERS, 128)
    high = found.astype(BF16)
    rest = found - high.astype(F32)
    middle = rest.astype(BF16)
    low = (rest - middle.astype(F32)).astype(BF16)
    parts = jnp.concatenate([high, middle, low], axis=0)
    slot = iota((128, 128), 0).astype(F32)
    line = iota((CLUSTERS, 128), 0)
    for r in range(LINES):
        chosen = jnp.where(slot == rank_of[r : r + 1, :], 1.0, 0.0).astype(BF16)
        taken = jnp.dot(parts, chosen, preferred_element_type=F32)
        taken = taken[0:CLUSTERS] + taken[CLUSTERS : 2 * CLUSTERS] + taken[2 * CLUSTERS :]
        out_ref[r : r + 1] = jnp.sum(
            jnp.where(line == cluster_ref[r : r + 1, :], taken, 0.0), axis=0, keepdims=True
        )


def local(embeds, cluster_of):
    dma = pltpu.SemaphoreType.DMA
    out = pl.pallas_call(
        kernel,
        out_shape=jax.ShapeDtypeStruct((LINES, 128), F32),
        in_specs=[pl.BlockSpec(memory_space=pl.ANY)] * 2,
        out_specs=pl.BlockSpec(memory_space=pltpu.VMEM),
        scratch_shapes=[
            pltpu.VMEM((LINES, 128), jnp.int32),
            pltpu.VMEM((DOCS, WIDTH), BF16),
            pltpu.VMEM((GROUP, DOCS), BF16),
            pltpu.VMEM((GROUP, WIDTH), F32),
            pltpu.VMEM((4 * SLOTS, WIDTH), BF16),
            pltpu.VMEM((MEMBERS, WIDTH), BF16),
            pltpu.VMEM((8, MEMBERS), F32),
            pltpu.VMEM((REGION, 128), F32),
            pltpu.VMEM((8, MEMBERS), F32),
            pltpu.VMEM((4, 8, 128), F32),
            pltpu.VMEM((4, 8, 128), F32),
            pltpu.VMEM((SIDE, 1, 128), F32),
            pltpu.VMEM((CLUSTERS, 1, 128), F32),
            pltpu.VMEM((LINES, 128), F32),
            pltpu.VMEM((2, len(DETOURS), PIECE, WIDTH), BF16),
            dma,
            dma((LOADS,)),
            dma((STAGES, SIDE)),
            dma((STAGES, SIDE)),
            dma((STAGES, SIDE, 2)),
            dma((STAGES, SIDE, 2)),
            dma((STAGES,)),
            dma((STAGES,)),
            dma((4,)),
            dma((4,)),
            dma((PLANES, SIDE)),
            dma,
            pltpu.SemaphoreType.REGULAR((STAGES,)),
            dma((2, len(DETOURS))),
            dma((2, len(DETOURS))),
            dma((2, len(DETOURS))),
        ],
        compiler_params=pltpu.CompilerParams(
            collective_id=0, has_side_effects=True, vmem_limit_bytes=53 * 2**20
        ),
        cost_estimate=pl.CostEstimate(flops=8 * 10**9, bytes_accessed=4 * 2**20, transcendentals=512),
    )(cluster_of.reshape(LINES, 128), embeds)
    return out.reshape(DOCS)


def solution(mesh):
    return jax.shard_map(
        local,
        mesh=mesh,
        in_specs=(P("docs", None), P("docs")),
        out_specs=P("docs"),
        check_vma=False,
    )
```
